256 devices in a mesh: seq: 64 (over x, y_lo, z), outer: 4 (over y_hi, core).
Axes of the slice: x: 4, y: 4 (y_hi: 2, y_lo: 2; y = y_hi * 2 + y_lo), z: 8, core: 2. Of those that a mesh axis runs over, the one named last changes fastest.
Arguments:
- queries: bfloat16 [65536, 1024], P(('seq', 'outer')), may hold values from -120 to 120
- keys: bfloat16 [65536, 1024], P(('seq', 'outer')), may hold values from -10 to 10
- values: bfloat16 [65536, 1024], P(('seq', 'outer')), may hold values from -10 to 10
- cotangent: bfloat16 [65536, 1024], P(('seq', 'outer')), may hold values from -6 to 6
Outputs:
- attended: bfloat16 [65536, 1024], P(('seq', 'outer'))
- grad_queries: float32 [65536, 1024], P(('seq', 'outer'))
- grad_keys: float32 [65536, 1024], P(('seq', 'outer'))
- grad_values: float32 [65536, 1024], P(('seq', 'outer'))
- summary_grad: float32 [256, 2048], P(('seq', 'outer'))
The draws below stay inside these ranges and needn't reach their ends.
All inputs are finite; a program needn't handle non-finite values.
Results may differ from the reference program's by a relative error of at most 0.01.
Values may be sent and summed in bfloat16 or wider, within the bound.
A program may use at most 128 MiB of HBM per device.

```python
import jax
import jax.numpy as jnp
from jax import lax

HEADS = 8
BLOCK = 128
ROWS = 256
SPANS = 256
TOKENS = 65536
WIDTH = 1024


def spread_rows(key):
    noise_key, offset_key = jax.random.split(key, 2)
    gauss = jnp.clip(jax.random.normal(noise_key, (TOKENS, WIDTH), jnp.float32), -6.0, 6.0)
    noise = gauss
    offsets = jnp.clip(jax.random.normal(offset_key, (TOKENS // ROWS, 1, WIDTH), jnp.float32), -4.0, 4.0)
    return (noise.reshape(TOKENS // ROWS, ROWS, WIDTH) + offsets).reshape(TOKENS, WIDTH)


def draw_keys(key, part):
    shared = spread_rows(key)
    return shared.astype(jnp.bfloat16)


def draw_queries(key, part):
    own_key = jax.random.fold_in(key, 5)
    result = jnp.clip(jax.random.normal(own_key, (TOKENS, WIDTH), jnp.float32), -6.0, 6.0)
    return result.astype(jnp.bfloat16)


def draw_values(key, part):
    key = jax.random.fold_in(key, 9)
    result = spread_rows(key)
    return result.astype(jnp.bfloat16)


def levels(rng, shape, cuts, low, largest):
    def one(position, shards_of):
        draws = jax.random.uniform(jax.random.fold_in(jax.random.fold_in(rng, 6), position), (shards_of,), jnp.float32, low / len(cuts), largest / len(cuts))
        return jnp.repeat(jnp.exp(draws), shape[position] // shards_of).reshape((-1,) + (1,) * (len(shape) - position - 1))

    level = one(*cuts[0])
    for cut in cuts[1:]:
        level = level * one(*cut)
    return level


def scatter_about(key, extent, width, bound, cuts=(), kind=jnp.bfloat16):
    level = levels(key, extent, cuts, -0.22, 0.18) if cuts else 1.0
    values = jax.random.normal(key, extent, jnp.float32) * width * level
    return jnp.minimum(jnp.maximum(values, -bound), bound).astype(kind)


def setup_inputs(seed: int = 0) -> dict:
    key_of = jax.random.split(jax.random.key(seed), 5)
    return {
        "queries": draw_queries(jax.random.fold_in(key_of[4], 71), 0),
        "keys": draw_keys(jax.random.fold_in(key_of[4], 71), 0),
        "values": draw_values(jax.random.fold_in(key_of[4], 71), 0),
        "cotangent": scatter_about(key_of[3], (TOKENS, WIDTH), 1.0, 6.0, ((0, 256),)),
    }


def halved(matrix):
    return (jnp.sum(matrix.reshape(matrix.shape[0] // 2, 2, matrix.shape[1]).astype(jnp.float32), axis=1) * 0.5).astype(jnp.bfloat16)


def doubled(matrix):
    return jnp.broadcast_to(matrix[:, None, :], (matrix.shape[0], 2, matrix.shape[1])).reshape(2 * matrix.shape[0], matrix.shape[1])


def attend(query_rows, key_sets, usable, cotangent):
    leaf_count, set_size, double_width = key_sets.shape
    feat_width = double_width // 2
    head_size = feat_width // HEADS
    leaf_rows = query_rows.shape[0] // leaf_count
    queries_h = query_rows.reshape(leaf_count, leaf_rows, HEADS, head_size).astype(jnp.float32)
    keys_h = key_sets[:, :, :feat_width].reshape(leaf_count, set_size, HEADS, head_size).astype(jnp.float32)
    values_h = key_sets[:, :, feat_width:].reshape(leaf_count, set_size, HEADS, head_size).astype(jnp.float32)
    cot_h = cotangent.reshape(leaf_count, leaf_rows, HEADS, head_size).astype(jnp.float32)
    score_scale = head_size ** -0.5
    scores = jnp.einsum("bqhe,bkhe->bhqk", queries_h, keys_h) * score_scale
    scores = jnp.where(usable[:, None, None, :], scores, -jnp.inf)
    highest = jnp.max(scores, axis=-1, keepdims=True)
    weights = jnp.exp(scores - highest)
    probs = weights / jnp.sum(weights, axis=-1, keepdims=True)
    probs_low = probs.astype(jnp.bfloat16)
    attended = jnp.einsum("bhqk,bkhe->bqhe", probs_low.astype(jnp.float32), values_h)
    dprobs = jnp.einsum("bqhe,bkhe->bhqk", cot_h, values_h)
    centre = jnp.sum(probs * dprobs, axis=-1, keepdims=True)
    dscores = (probs * (dprobs - centre)).astype(jnp.bfloat16).astype(jnp.float32)
    grad_q = jnp.einsum("bhqk,bkhe->bqhe", dscores, keys_h) * score_scale
    grad_k = jnp.einsum("bhqk,bqhe->bkhe", dscores, queries_h) * score_scale
    grad_v = jnp.einsum("bhqk,bqhe->bkhe", probs_low.astype(jnp.float32), cot_h)
    total_rows = leaf_count * leaf_rows
    set_grad = jnp.concatenate([grad_k.reshape(leaf_count, set_size, feat_width), grad_v.reshape(leaf_count, set_size, feat_width)], axis=-1)
    return attended.reshape(total_rows, feat_width).astype(jnp.bfloat16), grad_q.reshape(total_rows, feat_width), set_grad


def reference(queries, keys, values, cotangent):
    keyvals = jnp.concatenate([keys, values], axis=1)
    pairs = halved(keyvals)
    quads = halved(pairs)
    summaries = (jnp.sum(keyvals.reshape(SPANS, ROWS, 2 * WIDTH).astype(jnp.float32), axis=1) / ROWS).astype(jnp.bfloat16)
    padded = jnp.pad(keyvals, ((BLOCK, BLOCK), (0, 0)))
    positions = jnp.arange(5 * BLOCK + SPANS, dtype=jnp.int32)

    def device_step(state_in, span):
        tok_acc, pair_acc, quad_acc, summary_acc = state_in
        start = (span * ROWS).astype(jnp.int32)
        extended = lax.dynamic_slice(padded, (start, jnp.int32(0)), (4 * BLOCK, 2 * WIDTH))
        partner_row = (jnp.bitwise_xor(span, 1) * BLOCK).astype(jnp.int32)
        sibling_row = (jnp.bitwise_xor(span // 2, 1) * BLOCK).astype(jnp.int32)
        partner_rows = lax.dynamic_slice(pairs, (partner_row, jnp.int32(0)), (BLOCK, 2 * WIDTH))
        sibling_rows = lax.dynamic_slice(quads, (sibling_row, jnp.int32(0)), (BLOCK, 2 * WIDTH))
        far_keys = jnp.concatenate([partner_rows, sibling_rows, summaries], axis=0)
        near_keys = jnp.stack([extended[:3 * BLOCK], extended[BLOCK:]])
        key_sets = jnp.concatenate([near_keys, jnp.broadcast_to(far_keys[None], (2,) + far_keys.shape)], axis=1)
        covered = (positions >= 5 * BLOCK) & ((positions - 5 * BLOCK) // 4 == span // 4)
        usable = jnp.stack([((positions >= BLOCK) | (span > 0)) & ~covered, ((positions < 2 * BLOCK) | (positions >= 3 * BLOCK) | (span < SPANS - 1)) & ~covered])
        query_rows = lax.dynamic_slice(queries, (start, jnp.int32(0)), (ROWS, WIDTH))
        cot_rows = lax.dynamic_slice(cotangent, (start, jnp.int32(0)), (ROWS, WIDTH))
        attended, grad_q, set_grad = attend(query_rows, key_sets, usable, cot_rows)
        ext_grad = jnp.pad(set_grad[0, :3 * BLOCK], ((0, BLOCK), (0, 0))) + jnp.pad(set_grad[1, :3 * BLOCK], ((BLOCK, 0), (0, 0)))
        far_grad = set_grad[0, 3 * BLOCK:] + set_grad[1, 3 * BLOCK:]
        old_rows = lax.dynamic_slice(tok_acc, (start, jnp.int32(0)), (4 * BLOCK, 2 * WIDTH))
        tok_acc = lax.dynamic_update_slice(tok_acc, old_rows + ext_grad, (start, jnp.int32(0)))
        old_pairs = lax.dynamic_slice(pair_acc, (partner_row, jnp.int32(0)), (BLOCK, 2 * WIDTH))
        pair_acc = lax.dynamic_update_slice(pair_acc, old_pairs + far_grad[:BLOCK], (partner_row, jnp.int32(0)))
        old_quads = lax.dynamic_slice(quad_acc, (sibling_row, jnp.int32(0)), (BLOCK, 2 * WIDTH))
        quad_acc = lax.dynamic_update_slice(quad_acc, old_quads + far_grad[BLOCK:2 * BLOCK], (sibling_row, jnp.int32(0)))
        summary_acc = summary_acc + far_grad[2 * BLOCK:]
        return (tok_acc, pair_acc, quad_acc, summary_acc), (attended, grad_q)

    start_state = (jnp.zeros((TOKENS + 2 * BLOCK, 2 * WIDTH), jnp.float32), jnp.zeros((TOKENS // 2, 2 * WIDTH), jnp.float32), jnp.zeros((TOKENS // 4, 2 * WIDTH), jnp.float32), jnp.zeros((SPANS, 2 * WIDTH), jnp.float32))
    final_state, outputs = lax.scan(device_step, start_state, jnp.arange(SPANS, dtype=jnp.int32))
    tok_acc, pair_acc, quad_acc, summary_acc = final_state
    pair_total = pair_acc + 0.5 * doubled(quad_acc)
    token_grad = tok_acc[BLOCK:TOKENS + BLOCK] + 0.5 * doubled(pair_total)
    token_grad = (token_grad.reshape(SPANS, ROWS, 2 * WIDTH) + summary_acc[:, None, :] / ROWS).reshape(TOKENS, 2 * WIDTH)
    attended = outputs[0].reshape(TOKENS, WIDTH)
    grad_queries = outputs[1].reshape(TOKENS, WIDTH)
    return attended, grad_queries, token_grad[:, :WIDTH], token_grad[:, WIDTH:], summary_acc
```

```python
import functools

import jax
import jax.numpy as jnp
from jax import lax
from jax.experimental import pallas as pl
from jax.experimental.pallas import tpu as pltpu
from jax.sharding import PartitionSpec as P

HEADS = 8
HEAD = 128
LEAF = 128
SPANS = 256
STEPS = 8
PLANE = 32
GROUP = 8
POST_LAG = 2
JOIN_LAG = 4
SCALE = HEAD**-0.5
LOG2E = 1.4426950408889634
MESH = pl.DeviceIdType.MESH
BF16 = jnp.bfloat16
F32 = jnp.float32

SENDS = 11
(S_TILE, S_RIM, S_PAIR, S_QUAD, S_FWD, S_SUM, S_RGRAD, S_PGRAD, S_QGRAD, S_SGRAD, S_BACK) = range(SENDS)
RECVS = 9
(R_RIM, R_PAIR, R_QUAD, R_FWD, R_SUM, R_RGRAD, R_PGRAD, R_QGRAD, R_SGRAD) = range(RECVS)


def dot(a, b, contract):
    return lax.dot_general(a, b, ((contract[:1], contract[1:]), ((), ())), preferred_element_type=F32)


def kernel(
    q, k, v, cot, att, gq, gk, gv, sg,
    tiles_in, sums, rim, pairs, pairs_in, quads, quads_in,
    rgrad, rgrad_in, pgrad, pgrad_in, qkeep, qgrad, qgrad_in,
    sgrad, sgrad_in, stage, back, back_in,
    send, recv, plane_recv,
):
    seq, outer = lax.axis_index("seq"), lax.axis_index("outer")
    x, ylo, z = lax.div(seq, 16), lax.rem(lax.div(seq, 8), 2), lax.rem(seq, 8)
    yhi, core = lax.div(outer, 2), lax.rem(outer, 2)
    span = seq * 4 + outer
    member = z * 4 + ylo * 2 + yhi
    group = x * 2 + core

    def of_span(s):
        return (lax.div(s, 4), lax.rem(s, 4))

    def of_member(m):
        mz, mylo, myhi = lax.div(m, 4), lax.rem(lax.div(m, 2), 2), lax.rem(m, 2)
        return ((x * 2 + mylo) * 8 + mz, myhi * 2 + core)

    def of_group(g):
        gx, gcore = lax.div(g, 2), lax.rem(g, 2)
        return ((gx * 2 + ylo) * 8 + z, yhi * 2 + gcore)

    following = of_span(lax.rem(span + 1, SPANS))
    previous = of_span(lax.rem(span + SPANS - 1, SPANS))
    partner = (seq, yhi * 2 + 1 - core)
    sibling = (seq, (1 - yhi) * 2 + core)

    def post(src, dst, s, r, device):
        pltpu.make_async_remote_copy(
            src_ref=src, dst_ref=dst, send_sem=send.at[s], recv_sem=r, device_id=device, device_id_type=MESH
        ).start()

    def arrived(ref, sem):
        pltpu.make_async_copy(ref, ref, sem).wait()

    barrier = pltpu.get_barrier_semaphore()

    def greet(device):
        pl.semaphore_signal(barrier, inc=1, device_id=device, device_id_type=MESH)

    def greet_plane(d, carry):
        greet(of_member(lax.rem(member + d, PLANE)))
        return carry

    lax.fori_loop(1, PLANE, greet_plane, 0)
    for d in range(1, GROUP):
        greet(of_group(lax.rem(group + d, GROUP)))
    greet(following)
    greet(previous)

    def grid(rows, cols):
        return (
            lax.broadcasted_iota(jnp.int32, (rows, cols), 0),
            lax.broadcasted_iota(jnp.int32, (rows, cols), 1),
        )

    row, col = grid(128, 256)
    halve = jnp.where((col >> 1) == row, 0.5, 0.0).astype(BF16)
    row, col = grid(64, 128)
    halve_again = jnp.where((col >> 1) == row, 0.5, 0.0).astype(BF16)
    row, col = grid(256, 256)
    turn = jnp.where(col == ((row & 15) * 16 + (row >> 4)), 1.0, 0.0).astype(BF16)

    chunks = []
    for kv, ref in enumerate((k, v)):
        whole = ref[...]
        pair_rows = dot(halve, whole, (1, 0)).astype(BF16)
        quad_rows = dot(halve_again, pair_rows, (1, 0)).astype(BF16)
        mean = jnp.sum(whole.astype(F32), axis=0, keepdims=True) * (1.0 / 256)
        chunks += [mean[:, h * HEAD:(h + 1) * HEAD] for h in range(HEADS)]
        for t in range(STEPS):
            pairs[t, kv] = pair_rows[:, t * HEAD:(t + 1) * HEAD]
            quads[t, kv] = quad_rows[:, t * HEAD:(t + 1) * HEAD]
    tiles_in[member] = jnp.concatenate(chunks, axis=0).astype(BF16)

    pl.semaphore_wait(barrier, PLANE - 1 + GROUP - 1 + 2)

    def send_tile(d, carry):
        post(tiles_in.at[member], tiles_in.at[member], S_TILE, plane_recv.at[0], of_member(lax.rem(member + d, PLANE)))
        return carry

    lax.fori_loop(1, PLANE, send_tile, 0)

    def send_step(t, carry):
        cols = pl.ds(pl.multiple_of(t * HEAD, HEAD), HEAD)
        post(quads.at[t], quads_in.at[t, 0], S_QUAD, recv.at[R_QUAD, t], sibling)
        for kv, ref in enumerate((k, v)):
            post(ref.at[pl.ds(LEAF, LEAF), cols], rim.at[t, kv], S_RIM, recv.at[R_RIM, t], following)
            post(ref.at[pl.ds(0, LEAF), cols], rim.at[t, 2 + kv], S_RIM, recv.at[R_RIM, t], previous)
        post(pairs.at[t], pairs_in.at[t], S_PAIR, recv.at[R_PAIR, t], partner)
        return carry

    lax.fori_loop(0, STEPS, send_step, 0)

    arrived(tiles_in.at[pl.ds(0, PLANE - 1)], plane_recv.at[0])
    for part in range(2):
        turned = dot(turn, tiles_in[part * 16:(part + 1) * 16].reshape(256, HEAD), (1, 0)).astype(BF16)
        for t in range(STEPS):
            for kv in range(2):
                at = (kv * 8 + t) * 16
                sums[t, group, kv * 32 + part * 16:kv * 32 + (part + 1) * 16, :] = turned[at:at + 16]

    def send_sums(t, carry):
        for d in range(1, GROUP):
            post(
                sums.at[t, group], sums.at[t, group], S_SUM, recv.at[R_SUM, t],
                of_group(lax.rem(group + d, GROUP)),
            )
        return carry

    lax.fori_loop(0, STEPS, send_sums, 0)

    def forward_quads(t):
        arrived(quads_in.at[t, 0], recv.at[R_QUAD, t])
        post(quads_in.at[t, 0], quads_in.at[t, 1], S_FWD, recv.at[R_FWD, t], partner)

    forward_quads(0)

    row, col = grid(256, 256)
    covered = ((row >> 6) == x) & (((row & 31) >> 1) == z * 2 + ylo)
    row, col = grid(128, 256)
    absent = ((col < LEAF) & (span == 0)) | ((col >= LEAF) & (span == SPANS - 1))

    def compute(t):
        @pl.when(t + 1 < STEPS)
        def _():
            forward_quads(t + 1)

        arrived(rim.at[t], recv.at[R_RIM, t])
        arrived(pairs_in.at[t], recv.at[R_PAIR, t])
        arrived(quads_in.at[t, 1], recv.at[R_FWD, t])
        arrived(sums.at[t, pl.ds(0, GROUP - 1)], recv.at[R_SUM, t])
        cols = pl.ds(pl.multiple_of(t * HEAD, HEAD), HEAD)
        qh, ch = q[:, cols], cot[:, cols]

        def rows_of(kv, ref):
            return jnp.concatenate(
                [
                    ref[:, cols],
                    pairs_in[t, kv],
                    quads_in[t, 0, kv],
                    quads_in[t, 1, kv],
                    sums[t, :, kv * 32:(kv + 1) * 32, :].reshape(SPANS, HEAD),
                ],
                axis=0,
            )

        def against(main, left, right, other):
            at_rim = jnp.concatenate(
                [dot(left, other[:LEAF], (1, 1)), dot(right, other[LEAF:], (1, 1))], axis=1
            )
            return jnp.concatenate([dot(main, other, (1, 1)), at_rim], axis=0)

        def gathered(main, left, right, weights):
            total = dot(main, weights[:768], (0, 0))
            at_rim = jnp.concatenate(
                [dot(left, weights[768:, :LEAF], (0, 0)), dot(right, weights[768:, LEAF:], (0, 0))], axis=1
            )
            return (total + at_rim).T

        keys, values = rows_of(0, k), rows_of(1, v)
        key_l, value_l, key_r, value_r = rim[t, 0], rim[t, 1], rim[t, 2], rim[t, 3]
        scores = against(keys, key_l, key_r, qh)
        scores = jnp.concatenate(
            [
                scores[:512],
                jnp.where(covered, -1e30, scores[512:768]),
                jnp.where(absent, -1e30, scores[768:]),
            ],
            axis=0,
        )
        highest = jnp.max(scores, axis=0, keepdims=True)
        weights = jnp.exp2((scores - highest) * (SCALE * LOG2E))
        probs = weights * (1.0 / jnp.sum(weights, axis=0, keepdims=True))
        probs_low = probs.astype(BF16)
        dprobs = against(values, value_l, value_r, ch)
        centre = jnp.sum(probs * dprobs, axis=0, keepdims=True)
        dscores = (probs * (dprobs - centre)).astype(BF16)

        att[:, cols] = gathered(values, value_l, value_r, probs_low).astype(BF16)
        gq[:, cols] = gathered(keys, key_l, key_r, dscores) * SCALE

        for kv, (low, other, out, factor) in enumerate(((dscores, qh, gk, SCALE), (probs_low, ch, gv, 1.0))):
            main = dot(low[:768], other, (1, 0)) * factor
            out[:, cols] = main[:256]
            pgrad[t, kv, 0:128, :] = main[256:384].astype(BF16)
            qkeep[t, kv] = main[384:448]
            pgrad[t, kv, 128:192, :] = main[448:512].astype(BF16)
            sgrad[t, :, kv * 32:(kv + 1) * 32, :] = main[512:].astype(BF16).reshape(GROUP, 32, HEAD)
            rgrad[t, kv] = (dot(low[768:, :LEAF], other[:LEAF], (1, 0)) * factor).astype(BF16)
            rgrad[t, 2 + kv] = (dot(low[768:, LEAF:], other[LEAF:], (1, 0)) * factor).astype(BF16)

        post(pgrad.at[t], pgrad_in.at[t], S_PGRAD, recv.at[R_PGRAD, t], partner)
        two = pl.ds(0, 2)
        other_two = pl.ds(2, 2)
        post(rgrad.at[t, two], rgrad_in.at[t, other_two], S_RGRAD, recv.at[R_RGRAD, t], previous)
        post(rgrad.at[t, other_two], rgrad_in.at[t, two], S_RGRAD, recv.at[R_RGRAD, t], following)
        for d in range(1, GROUP):
            there = lax.rem(group + d, GROUP)
            post(sgrad.at[t, there], sgrad_in.at[t, group], S_SGRAD, recv.at[R_SGRAD, t], of_group(there))
        sgrad_in[t, group] = sgrad[t, group]

    def reduce(t):
        arrived(pgrad_in.at[t], recv.at[R_PGRAD, t])
        qgrad[t] = (qkeep[t] + pgrad_in[t, :, 128:192, :].astype(F32)).astype(BF16)
        post(qgrad.at[t], qgrad_in.at[t], S_QGRAD, recv.at[R_QGRAD, t], sibling)
        arrived(sgrad_in.at[t, pl.ds(0, GROUP - 1)], recv.at[R_SGRAD, t])
        total = sgrad_in[t, 0].astype(F32)
        for g in range(1, GROUP):
            total = total + sgrad_in[t, g].astype(F32)
        total = total.astype(BF16)
        for kv in range(2):
            for part in range(2):
                at = kv * 32 + part * 16
                stage[part, kv * 8 + t] = total[at:at + 16]

    row, col = grid(256, 128)
    double = jnp.where((row >> 1) == col, 0.5, 0.0).astype(BF16)
    row, col = grid(256, 64)
    double_twice = jnp.where((row >> 2) == col, 0.25, 0.0).astype(BF16)

    def join(t):
        arrived(rgrad_in.at[t], recv.at[R_RGRAD, t])
        arrived(qgrad_in.at[t], recv.at[R_QGRAD, t])
        cols = pl.ds(pl.multiple_of(t * HEAD, HEAD), HEAD)
        for kv, out in enumerate((gk, gv)):
            ends = jnp.concatenate([rgrad_in[t, kv], rgrad_in[t, 2 + kv]], axis=0).astype(F32)
            coarse = dot(double, pgrad_in[t, kv, 0:128, :], (1, 0)) + dot(double_twice, qgrad_in[t, kv], (1, 0))
            out[:, cols] = out[:, cols] + ends + coarse

    def step(t, carry):
        compute(t)

        @pl.when(t >= POST_LAG)
        def _():
            reduce(t - POST_LAG)

        @pl.when(t >= JOIN_LAG)
        def _():
            join(t - JOIN_LAG)

        return carry

    def repeat(f):
        def body(t, carry):
            f(t)
            return carry

        return body

    lax.fori_loop(0, STEPS, step, 0)
    lax.fori_loop(STEPS - POST_LAG, STEPS, repeat(reduce), 0)

    for part in range(2):
        turned = dot(turn, stage[part].reshape(256, HEAD), (1, 0)).astype(BF16)
        back[part * 16:(part + 1) * 16] = turned.reshape(16, 16, HEAD)

    back_in[member] = back[member]

    def send_back(d, carry):
        there = lax.rem(member + d, PLANE)
        post(back.at[there], back_in.at[member], S_BACK, plane_recv.at[1], of_member(there))
        return carry

    lax.fori_loop(1, PLANE, send_back, 0)
    lax.fori_loop(STEPS - JOIN_LAG, STEPS, repeat(join), 0)

    arrived(back_in.at[pl.ds(0, PLANE - 1)], plane_recv.at[1])
    total = back_in[0].astype(F32)
    for m in range(1, PLANE):
        total = total + back_in[m].astype(F32)
    for kv, out in enumerate((gk, gv)):
        for h in range(HEADS):
            row = total[kv * 8 + h:kv * 8 + h + 1]
            sg[:, (kv * 8 + h) * HEAD:(kv * 8 + h + 1) * HEAD] = row
            out[:, h * HEAD:(h + 1) * HEAD] = out[:, h * HEAD:(h + 1) * HEAD] + row * (1.0 / 256)

    arrived(tiles_in.at[pl.ds(0, PLANE - 1)], send.at[S_TILE])
    arrived(rim, send.at[S_RIM])
    arrived(pairs, send.at[S_PAIR])
    arrived(quads, send.at[S_QUAD])
    arrived(quads, send.at[S_FWD])
    arrived(sums.at[:, pl.ds(0, GROUP - 1)], send.at[S_SUM])
    arrived(rgrad, send.at[S_RGRAD])
    arrived(pgrad, send.at[S_PGRAD])
    arrived(qgrad, send.at[S_QGRAD])
    arrived(sgrad.at[:, pl.ds(0, GROUP - 1)], send.at[S_SGRAD])
    arrived(back.at[pl.ds(0, PLANE - 1)], send.at[S_BACK])


def on_device(queries, keys, values, cotangent):
    rows, width = queries.shape
    in_vmem = pl.BlockSpec(memory_space=pltpu.VMEM)
    block = (STEPS, 4, LEAF, HEAD)
    return pl.pallas_call(
        kernel,
        out_shape=(
            jax.ShapeDtypeStruct((rows, width), BF16),
            jax.ShapeDtypeStruct((rows, width), F32),
            jax.ShapeDtypeStruct((rows, width), F32),
            jax.ShapeDtypeStruct((rows, width), F32),
            jax.ShapeDtypeStruct((1, 2 * width), F32),
        ),
        in_specs=[in_vmem] * 4,
        out_specs=(in_vmem,) * 5,
        scratch_shapes=[
            pltpu.VMEM((PLANE, 16, HEAD), BF16),
            pltpu.VMEM((STEPS, GROUP, 64, HEAD), BF16),
            pltpu.VMEM(block, BF16),
            pltpu.VMEM((STEPS, 2, 128, HEAD), BF16),
            pltpu.VMEM((STEPS, 2, 128, HEAD), BF16),
            pltpu.VMEM((STEPS, 2, 64, HEAD), BF16),
            pltpu.VMEM((STEPS, 2, 2, 64, HEAD), BF16),
            pltpu.VMEM(block, BF16),
            pltpu.VMEM(block, BF16),
            pltpu.VMEM((STEPS, 2, 192, HEAD), BF16),
            pltpu.VMEM((STEPS, 2, 192, HEAD), BF16),
            pltpu.VMEM((STEPS, 2, 64, HEAD), F32),
            pltpu.VMEM((STEPS, 2, 64, HEAD), BF16),
            pltpu.VMEM((STEPS, 2, 64, HEAD), BF16),
            pltpu.VMEM((STEPS, GROUP, 64, HEAD), BF16),
            pltpu.VMEM((STEPS, GROUP, 64, HEAD), BF16),
            pltpu.VMEM((2, 16, 16, HEAD), BF16),
            pltpu.VMEM((PLANE, 16, HEAD), BF16),
            pltpu.VMEM((PLANE, 16, HEAD), BF16),
            pltpu.SemaphoreType.DMA((SENDS,)),
            pltpu.SemaphoreType.DMA((RECVS, STEPS)),
            pltpu.SemaphoreType.DMA((2,)),
        ],
        compiler_params=pltpu.CompilerParams(
            collective_id=0, has_side_effects=True, vmem_limit_bytes=48 * 2**20
        ),
        name="attend",
    )(queries, keys, values, cotangent)


def solution(mesh):
    spec = P(("seq", "outer"), None)
    return jax.shard_map(
        on_device, mesh=mesh, in_specs=(spec,) * 4, out_specs=(spec,) * 5, check_vma=False
    )
```

```python
import functools

import jax
import jax.numpy as jnp
from jax import lax
from jax.experimental import pallas as pl
from jax.experimental.pallas import tpu as pltpu
from jax.sharding import PartitionSpec as P

HEADS = 8
HEAD = 128
LEAF = 128
SPANS = 256
STEPS = 8
PLANE = 32
ZS, YS, XS = 8, 4, 4
GROUP = 2 * XS
HALF_LAG = 2
POST_LAG = 5
SCALE = HEAD**-0.5
LOG2E = 1.4426950408889634
MESH = pl.DeviceIdType.MESH
BF16 = jnp.bfloat16
F32 = jnp.float32

(
    S_TILE, S_RIM, S_PAIR, S_QUAD, S_QFWD, S_SUM, S_RGRAD, S_PGRAD, S_QGRAD, S_SGRAD, S_BACK,
) = range(11)
R_RIM, R_PAIR, R_QUAD, R_QFWD, R_SUM, R_RGRAD, R_PGRAD, R_QGRAD, R_SGRAD = range(9)


def dot(a, b, contract):
    return lax.dot_general(a, b, ((contract[:1], contract[1:]), ((), ())), preferred_element_type=F32)


def kernel(
    q_in, k_in, v_in, cot_in, att_out, gq_out, gk_out, gv_out, sg_out,
    q, k, v, cot, att, gq, gk, gv, sg,
    tiles_in, sums, rim, pairs, pairs_in, quads, quads_in,
    rgrad, rgrad_in, pgrad, pgrad_in, qkeep, qgrad, qgrad_in,
    sgrad, sgrad_in, probs_kept, dscores_kept, stage, back, back_in,
    send, recv, plane_recv, load, store,
):
    seq, outer = lax.axis_index("seq"), lax.axis_index("outer")
    x, ylo, z = lax.div(seq, 16), lax.rem(lax.div(seq, 8), 2), lax.rem(seq, 8)
    yhi, core = lax.div(outer, 2), lax.rem(outer, 2)
    span = seq * 4 + outer
    y = ylo * 2 + yhi
    member = z * 4 + y

    def at(x, y, z):
        return ((x * 2 + lax.div(y, 2)) * 8 + z, lax.rem(y, 2) * 2 + core)

    def of_span(s):
        return (lax.div(s, 4), lax.rem(s, 4))

    following = of_span(lax.rem(span + 1, SPANS))
    previous = of_span(lax.rem(span + SPANS - 1, SPANS))
    partner = (seq, yhi * 2 + 1 - core)
    sibling = (seq, (1 - yhi) * 2 + core)
    plane = [
        (lax.rem(z + dz, ZS) * YS + lax.rem(y + dy, YS), at(x, lax.rem(y + dy, YS), lax.rem(z + dz, ZS)))
        for dz in (4, 3, 5, 2, 6, 1, 7, 0)
        for dy in (2, 1, 3, 0)
        if dz or dy
    ]
    group = core * XS + x
    mates = []
    for dx, dcore in ((2, 0), (2, 1), (1, 0), (3, 0), (1, 1), (3, 1), (0, 1)):
        mx, mcore = lax.rem(x + dx, XS), lax.rem(core + dcore, 2)
        mates.append((mcore * XS + mx, ((mx * 2 + ylo) * 8 + z, yhi * 2 + mcore)))

    loads = [
        pltpu.make_async_copy(src, dst, load.at[i])
        for i, (src, dst) in enumerate(((k_in, k), (v_in, v), (q_in, q), (cot_in, cot)))
    ]
    for copy in loads:
        copy.start()

    def post(src, dst, s, r, device):
        pltpu.make_async_remote_copy(
            src_ref=src, dst_ref=dst, send_sem=send.at[s], recv_sem=r, device_id=device, device_id_type=MESH
        ).start()

    def arrived(ref, sem):
        pltpu.make_async_copy(ref, ref, sem).wait()

    barrier = pltpu.get_barrier_semaphore()

    def greet(device):
        pl.semaphore_signal(barrier, inc=1, device_id=device, device_id_type=MESH)

    for _, device in plane + mates:
        greet(device)
    greet(following)
    greet(previous)

    def grid(rows, cols):
        return (
            lax.broadcasted_iota(jnp.int32, (rows, cols), 0),
            lax.broadcasted_iota(jnp.int32, (rows, cols), 1),
        )

    row, col = grid(128, 256)
    halve = jnp.where((col >> 1) == row, 0.5, 0.0).astype(BF16)
    row, col = grid(64, 128)
    halve_again = jnp.where((col >> 1) == row, 0.5, 0.0).astype(BF16)
    row, col = grid(256, 256)
    turn = jnp.where(col == ((row & 15) * 16 + (row >> 4)), 1.0, 0.0).astype(BF16)

    loads[0].wait()
    loads[1].wait()
    chunks = []
    for kv, ref in enumerate((k, v)):
        whole = ref[...]
        pair_rows = dot(halve, whole, (1, 0)).astype(BF16)
        quad_rows = dot(halve_again, pair_rows, (1, 0)).astype(BF16)
        mean = jnp.sum(whole.astype(F32), axis=0, keepdims=True) * (1.0 / 256)
        chunks += [mean[:, h * HEAD:(h + 1) * HEAD] for h in range(HEADS)]
        for t in range(STEPS):
            pairs[t, kv] = pair_rows[:, t * HEAD:(t + 1) * HEAD]
            quads[t, kv] = quad_rows[:, t * HEAD:(t + 1) * HEAD]
    tiles_in[member] = jnp.concatenate(chunks, axis=0).astype(BF16)

    pl.semaphore_wait(barrier, len(plane) + len(mates) + 2)

    for _, device in plane:
        post(tiles_in.at[member], tiles_in.at[member], S_TILE, plane_recv.at[0], device)

    def send_step(t, carry):
        cols = pl.ds(pl.multiple_of(t * HEAD, HEAD), HEAD)
        post(quads.at[t], quads_in.at[t, 0], S_QUAD, recv.at[R_QUAD, t], sibling)
        for kv, ref in enumerate((k_in, v_in)):
            post(ref.at[pl.ds(LEAF, LEAF), cols], rim.at[t, kv], S_RIM, recv.at[R_RIM, t], following)
            post(ref.at[pl.ds(0, LEAF), cols], rim.at[t, 2 + kv], S_RIM, recv.at[R_RIM, t], previous)
        post(pairs.at[t], pairs_in.at[t], S_PAIR, recv.at[R_PAIR, t], partner)
        return carry

    lax.fori_loop(0, STEPS, send_step, 0)

    arrived(tiles_in.at[pl.ds(0, PLANE - 1)], plane_recv.at[0])
    for part in range(2):
        turned = dot(turn, tiles_in[part * 16:(part + 1) * 16].reshape(256, HEAD), (1, 0)).astype(BF16)
        for t in range(STEPS):
            for kv in range(2):
                first = (kv * 8 + t) * 16
                sums[t, group, kv * 32 + part * 16:kv * 32 + (part + 1) * 16, :] = turned[first:first + 16]

    def send_sums(t, carry):
        for _, device in mates:
            post(sums.at[t, group], sums.at[t, group], S_SUM, recv.at[R_SUM, t], device)
        return carry

    lax.fori_loop(0, STEPS, send_sums, 0)

    def forward(t):
        arrived(quads_in.at[t, 0], recv.at[R_QUAD, t])
        post(quads_in.at[t, 0], quads_in.at[t, 1], S_QFWD, recv.at[R_QFWD, t], partner)

    forward(0)
    loads[2].wait()
    loads[3].wait()

    row, col = grid(256, 256)
    covered = (((row >> 5) & 3) == x) & (((row & 31) >> 1) == z * 2 + ylo)
    row, col = grid(128, 256)
    absent = ((col < LEAF) & (span == 0)) | ((col >= LEAF) & (span == SPANS - 1))

    def columns(t):
        return pl.ds(pl.multiple_of(t * HEAD, HEAD), HEAD)

    def rows_of(t, kv, ref):
        return jnp.concatenate(
            [
                ref[:, columns(t)],
                pairs_in[t, kv],
                quads_in[t, 0, kv],
                quads_in[t, 1, kv],
                sums[t, :, kv * 32:(kv + 1) * 32, :].reshape(SPANS, HEAD),
            ],
            axis=0,
        )

    def compute(t):
        @pl.when(t + 1 < STEPS)
        def _():
            forward(t + 1)

        arrived(rim.at[t], recv.at[R_RIM, t])
        arrived(pairs_in.at[t], recv.at[R_PAIR, t])
        arrived(quads_in.at[t, 1], recv.at[R_QFWD, t])
        arrived(sums.at[t, pl.ds(0, GROUP - 1)], recv.at[R_SUM, t])
        cols = columns(t)
        qh, ch = q[:, cols], cot[:, cols]

        def against(main, left, right, other):
            at_rim = jnp.concatenate(
                [dot(left, other[:LEAF], (1, 1)), dot(right, other[LEAF:], (1, 1))], axis=1
            )
            return jnp.concatenate([dot(main, other, (1, 1)), at_rim], axis=0)

        keys, values = rows_of(t, 0, k), rows_of(t, 1, v)
        key_l, value_l, key_r, value_r = rim[t, 0], rim[t, 1], rim[t, 2], rim[t, 3]
        scores = against(keys, key_l, key_r, qh)
        scores = jnp.concatenate(
            [
                scores[:512],
                jnp.where(covered, -1e30, scores[512:768]),
                jnp.where(absent, -1e30, scores[768:]),
            ],
            axis=0,
        )
        highest = jnp.max(scores, axis=0, keepdims=True)
        weights = jnp.exp2((scores - highest) * (SCALE * LOG2E))
        probs = weights * (1.0 / jnp.sum(weights, axis=0, keepdims=True))
        probs_low = probs.astype(BF16)
        dprobs = against(values, value_l, value_r, ch)
        centre = jnp.sum(probs * dprobs, axis=0, keepdims=True)
        dscores = (probs * (dprobs - centre)).astype(BF16)

        probs_kept[t] = probs_low
        dscores_kept[t] = dscores

        sides = ((dscores, qh, SCALE), (probs_low, ch, 1.0))
        for kv, (low, other, factor) in enumerate(sides):
            far = (dot(low[512:768], other, (1, 0)) * factor).astype(BF16)
            sgrad[t, :, kv * 32:(kv + 1) * 32, :] = far.reshape(GROUP, 32, HEAD)
        for there, device in mates:
            post(sgrad.at[t, there], sgrad_in.at[t, group], S_SGRAD, recv.at[R_SGRAD, t], device)
        sgrad_in[t, group] = sgrad[t, group]

        for kv, (low, other, factor) in enumerate(sides):
            rgrad[t, kv] = (dot(low[768:, :LEAF], other[:LEAF], (1, 0)) * factor).astype(BF16)
            rgrad[t, 2 + kv] = (dot(low[768:, LEAF:], other[LEAF:], (1, 0)) * factor).astype(BF16)
        two, other_two = pl.ds(0, 2), pl.ds(2, 2)
        post(rgrad.at[t, two], rgrad_in.at[t, other_two], S_RGRAD, recv.at[R_RGRAD, t], previous)
        post(rgrad.at[t, other_two], rgrad_in.at[t, two], S_RGRAD, recv.at[R_RGRAD, t], following)

        for kv, (low, other, factor) in enumerate(sides):
            coarse = dot(low[256:512], other, (1, 0)) * factor
            pgrad[t, kv, 0:128, :] = coarse[:128].astype(BF16)
            qkeep[t, kv] = coarse[128:192]
            pgrad[t, kv, 128:192, :] = coarse[192:].astype(BF16)
        post(pgrad.at[t], pgrad_in.at[t], S_PGRAD, recv.at[R_PGRAD, t], partner)

    def gathered(t, kv, ref, weights):
        total = dot(rows_of(t, kv, ref), weights[:768], (0, 0))
        at_rim = jnp.concatenate(
            [
                dot(rim[t, kv], weights[768:, :LEAF], (0, 0)),
                dot(rim[t, 2 + kv], weights[768:, LEAF:], (0, 0)),
            ],
            axis=1,
        )
        return (total + at_rim).T

    def gather(t):
        att[:, columns(t)] = gathered(t, 1, v, probs_kept[t]).astype(BF16)
        gq[:, columns(t)] = gathered(t, 0, k, dscores_kept[t]) * SCALE

    def halves(t):
        arrived(pgrad_in.at[t], recv.at[R_PGRAD, t])
        qgrad[t] = (qkeep[t] + pgrad_in[t, :, 128:192, :].astype(F32)).astype(BF16)
        post(qgrad.at[t], qgrad_in.at[t], S_QGRAD, recv.at[R_QGRAD, t], sibling)

    def reduce(t):
        arrived(sgrad_in.at[t, pl.ds(0, GROUP - 1)], recv.at[R_SGRAD, t])
        total = jnp.sum(sgrad_in[t].astype(F32), axis=0).astype(BF16)
        for kv in range(2):
            for part in range(2):
                first = kv * 32 + part * 16
                stage[part, kv * 8 + t] = total[first:first + 16]

    row, col = grid(256, 128)
    double = jnp.where((row >> 1) == col, 0.5, 0.0).astype(BF16)
    row, col = grid(256, 64)
    double_twice = jnp.where((row >> 2) == col, 0.25, 0.0).astype(BF16)

    def join(t):
        arrived(rgrad_in.at[t], recv.at[R_RGRAD, t])
        arrived(qgrad_in.at[t], recv.at[R_QGRAD, t])
        cols = columns(t)
        sides = ((dscores_kept, q, gk, gk_out, SCALE), (probs_kept, cot, gv, gv_out, 1.0))
        for kv, (low, other, out, out_hbm, factor) in enumerate(sides):
            own = dot(low[t, 0:256, :], other[:, cols], (1, 0)) * factor
            ends = jnp.concatenate([rgrad_in[t, kv], rgrad_in[t, 2 + kv]], axis=0).astype(F32)
            coarse = dot(double, pgrad_in[t, kv, 0:128, :], (1, 0)) + dot(double_twice, qgrad_in[t, kv], (1, 0))
            out[:, cols] = own + ends + coarse
            pltpu.make_async_copy(out.at[:, cols], out_hbm.at[:, cols], store.at[kv]).start()

    def step(t, carry):
        compute(t)

        @pl.when(t >= HALF_LAG)
        def _():
            halves(t - HALF_LAG)

        @pl.when(t >= POST_LAG)
        def _():
            reduce(t - POST_LAG)

        return carry

    def repeat(f):
        def body(t, carry):
            f(t)
            return carry

        return body

    lax.fori_loop(0, STEPS, step, 0)
    lax.fori_loop(STEPS - HALF_LAG, STEPS, repeat(halves), 0)
    lax.fori_loop(STEPS - POST_LAG, STEPS, repeat(reduce), 0)

    for part in range(2):
        turned = dot(turn, stage[part].reshape(256, HEAD), (1, 0)).astype(BF16)
        back[part * 16:(part + 1) * 16] = turned.reshape(16, 16, HEAD)
    for there, device in plane:
        post(back.at[there], back_in.at[member], S_BACK, plane_recv.at[1], device)
    back_in[member] = back[member]

    lax.fori_loop(0, STEPS, repeat(gather), 0)
    stores = [
        pltpu.make_async_copy(src, dst, store.at[2 + i])
        for i, (src, dst) in enumerate(((att, att_out), (gq, gq_out), (sg, sg_out)))
    ]
    stores[0].start()
    stores[1].start()
    lax.fori_loop(0, STEPS, repeat(join), 0)
    arrived(back_in.at[pl.ds(0, PLANE - 1)], plane_recv.at[1])
    total = jnp.sum(back_in[...].astype(F32), axis=0)
    for c in range(2 * HEADS):
        sg[:, c * HEAD:(c + 1) * HEAD] = total[c:c + 1]
    stores[2].start()

    arrived(tiles_in.at[pl.ds(0, PLANE - 1)], send.at[S_TILE])
    arrived(rim, send.at[S_RIM])
    arrived(pairs, send.at[S_PAIR])
    arrived(quads, send.at[S_QUAD])
    arrived(quads, send.at[S_QFWD])
    arrived(sums.at[:, pl.ds(0, GROUP - 1)], send.at[S_SUM])
    arrived(rgrad, send.at[S_RGRAD])
    arrived(pgrad, send.at[S_PGRAD])
    arrived(qgrad, send.at[S_QGRAD])
    arrived(sgrad.at[:, pl.ds(0, GROUP - 1)], send.at[S_SGRAD])
    arrived(back.at[pl.ds(0, PLANE - 1)], send.at[S_BACK])
    arrived(gk, store.at[0])
    arrived(gv, store.at[1])
    for copy in stores:
        copy.wait()


def finish(att, gq, gk, gv, sg, att_out, gq_out, gk_out, gv_out, sg_out, kept, low, row, load, store):
    through = ((sg, row, sg_out), (gk, kept.at[0], gk_out), (gv, kept.at[1], gv_out), (gq, kept.at[2], gq_out), (att, low, att_out))
    loads = [pltpu.make_async_copy(src, via, load.at[i]) for i, (src, via, _) in enumerate(through)]
    stores = [pltpu.make_async_copy(via, dst, store.at[i]) for i, (_, via, dst) in enumerate(through)]
    for copy in loads:
        copy.start()
    width = kept.shape[2]
    for i in range(5):
        loads[i].wait()
        if i in (1, 2):
            kept[i - 1] = kept[i - 1] + row[:, (i - 1) * width:i * width] * (1.0 / 256)
        stores[i].start()
    for copy in stores:
        copy.wait()


def on_device(queries, keys, values, cotangent):
    rows, width = queries.shape
    in_vmem = pl.BlockSpec(memory_space=pltpu.VMEM)
    in_hbm = pl.BlockSpec(memory_space=pltpu.HBM)
    out_shape = (
        jax.ShapeDtypeStruct((rows, width), BF16),
        jax.ShapeDtypeStruct((rows, width), F32),
        jax.ShapeDtypeStruct((rows, width), F32),
        jax.ShapeDtypeStruct((rows, width), F32),
        jax.ShapeDtypeStruct((1, 2 * width), F32),
    )
    block = (STEPS, 4, LEAF, HEAD)
    parts = pl.pallas_call(
        kernel,
        out_shape=out_shape,
        in_specs=[in_hbm] * 4,
        out_specs=(in_hbm,) * 5,
        scratch_shapes=[pltpu.VMEM((rows, width), BF16)] * 5 + [pltpu.VMEM((rows, width), F32)] * 3 + [
            pltpu.VMEM((1, 2 * width), F32),
            pltpu.VMEM((PLANE, 16, HEAD), BF16),
            pltpu.VMEM((STEPS, GROUP, 64, HEAD), BF16),
            pltpu.VMEM(block, BF16),
            pltpu.VMEM((STEPS, 2, 128, HEAD), BF16),
            pltpu.VMEM((STEPS, 2, 128, HEAD), BF16),
            pltpu.VMEM((STEPS, 2, 64, HEAD), BF16),
            pltpu.VMEM((STEPS, 2, 2, 64, HEAD), BF16),
            pltpu.VMEM(block, BF16),
            pltpu.VMEM(block, BF16),
            pltpu.VMEM((STEPS, 2, 192, HEAD), BF16),
            pltpu.VMEM((STEPS, 2, 192, HEAD), BF16),
            pltpu.VMEM((STEPS, 2, 64, HEAD), F32),
            pltpu.VMEM((STEPS, 2, 64, HEAD), BF16),
            pltpu.VMEM((STEPS, 2, 64, HEAD), BF16),
            pltpu.VMEM((STEPS, GROUP, 64, HEAD), BF16),
            pltpu.VMEM((STEPS, GROUP, 64, HEAD), BF16),
            pltpu.VMEM((STEPS, 896, 256), BF16),
            pltpu.VMEM((STEPS, 896, 256), BF16),
            pltpu.VMEM((2, 16, 16, HEAD), BF16),
            pltpu.VMEM((PLANE, 16, HEAD), BF16),
            pltpu.VMEM((PLANE, 16, HEAD), BF16),
            pltpu.SemaphoreType.DMA((11,)),
            pltpu.SemaphoreType.DMA((9, STEPS)),
            pltpu.SemaphoreType.DMA((2,)),
            pltpu.SemaphoreType.DMA((4,)),
            pltpu.SemaphoreType.DMA((5,)),
        ],
        compiler_params=pltpu.CompilerParams(
            collective_id=0, has_side_effects=True, vmem_limit_bytes=62 * 2**20
        ),
        name="attend",
    )(queries, keys, values, cotangent)
    return pl.pallas_call(
        finish,
        out_shape=out_shape,
        in_specs=[in_hbm] * 5,
        out_specs=(in_hbm,) * 5,
        scratch_shapes=[
            pltpu.VMEM((3, rows, width), F32),
            pltpu.VMEM((rows, width), BF16),
            pltpu.VMEM((1, 2 * width), F32),
            pltpu.SemaphoreType.DMA((5,)),
            pltpu.SemaphoreType.DMA((5,)),
        ],
        compiler_params=pltpu.CompilerParams(vmem_limit_bytes=62 * 2**20),
        name="finish",
    )(*parts)


def solution(mesh):
    spec = P(("seq", "outer"), None)
    return jax.shard_map(
        on_device, mesh=mesh, in_specs=(spec,) * 4, out_specs=(spec,) * 5, check_vma=False
    )
```

```python
import functools

import jax
import jax.numpy as jnp
from jax import lax
from jax.experimental import pallas as pl
from jax.experimental.pallas import tpu as pltpu
from jax.sharding import PartitionSpec as P

HEADS = 8
HEAD = 128
LEAF = 128
SPANS = 256
STEPS = 8
PLANE = 32
ZS, YS, XS = 8, 4, 4
GROUP = 2 * XS
HOLD = 3
HALF_LAG = 2
POST_LAG = 5
SCALE = HEAD**-0.5
LOG2E = 1.4426950408889634
MESH = pl.DeviceIdType.MESH
BF16 = jnp.bfloat16
F32 = jnp.float32

(
    S_TILE, S_RIM, S_PAIR, S_QUAD, S_QFWD, S_SUM, S_RGRAD, S_PGRAD, S_QGRAD, S_SGRAD, S_BACK,
) = range(11)
R_RIM, R_PAIR, R_QUAD, R_QFWD, R_SUM, R_RGRAD, R_PGRAD, R_QGRAD, R_SGRAD = range(9)


def dot(a, b, contract):
    return lax.dot_general(a, b, ((contract[:1], contract[1:]), ((), ())), preferred_element_type=F32)


def kernel(
    q_in, k_in, v_in, cot_in,
    att0, att1, gq0, gq1, gq2, gq3, gk0, gk1, gk2, gk3, gv0, gv1, gv2, gv3, sg,
    q, k, v, cot,
    tiles_in, sums, rim, pairs, pairs_in, quads, quads_in,
    rgrad, rgrad_in, pgrad, pgrad_in, qkeep, qgrad, qgrad_in,
    sgrad, sgrad_in, probs_kept, dscores_kept, stage, back, back_in,
    send, recv, plane_recv, load,
):
    seq, outer = lax.axis_index("seq"), lax.axis_index("outer")
    x, ylo, z = lax.div(seq, 16), lax.rem(lax.div(seq, 8), 2), lax.rem(seq, 8)
    yhi, core = lax.div(outer, 2), lax.rem(outer, 2)
    span = seq * 4 + outer
    y = ylo * 2 + yhi
    member = z * 4 + y

    def at(x, y, z):
        return ((x * 2 + lax.div(y, 2)) * 8 + z, lax.rem(y, 2) * 2 + core)

    def of_span(s):
        return (lax.div(s, 4), lax.rem(s, 4))

    following = of_span(lax.rem(span + 1, SPANS))
    previous = of_span(lax.rem(span + SPANS - 1, SPANS))
    partner = (seq, yhi * 2 + 1 - core)
    sibling = (seq, (1 - yhi) * 2 + core)
    plane = [
        (lax.rem(z + dz, ZS) * YS + lax.rem(y + dy, YS), at(x, lax.rem(y + dy, YS), lax.rem(z + dz, ZS)))
        for dz in (4, 3, 5, 2, 6, 1, 7, 0)
        for dy in (2, 1, 3, 0)
        if dz or dy
    ]
    group = core * XS + x
    mates = []
    for dx, dcore in ((2, 0), (2, 1), (1, 0), (3, 0), (1, 1), (3, 1), (0, 1)):
        mx, mcore = lax.rem(x + dx, XS), lax.rem(core + dcore, 2)
        mates.append((mcore * XS + mx, ((mx * 2 + ylo) * 8 + z, yhi * 2 + mcore)))

    loads = [
        pltpu.make_async_copy(src, dst, load.at[i])
        for i, (src, dst) in enumerate(((k_in, k), (v_in, v), (q_in, q), (cot_in, cot)))
    ]
    for copy in loads:
        copy.start()

    def post(src, dst, s, r, device):
        pltpu.make_async_remote_copy(
            src_ref=src, dst_ref=dst, send_sem=send.at[s], recv_sem=r, device_id=device, device_id_type=MESH
        ).start()

    def arrived(ref, sem):
        pltpu.make_async_copy(ref, ref, sem).wait()

    barrier = pltpu.get_barrier_semaphore()

    def greet(device):
        pl.semaphore_signal(barrier, inc=1, device_id=device, device_id_type=MESH)

    for _, device in plane + mates:
        greet(device)
    greet(following)
    greet(previous)

    def grid(rows, cols):
        return (
            lax.broadcasted_iota(jnp.int32, (rows, cols), 0),
            lax.broadcasted_iota(jnp.int32, (rows, cols), 1),
        )

    row, col = grid(128, 256)
    halve = jnp.where((col >> 1) == row, 0.5, 0.0).astype(BF16)
    row, col = grid(64, 128)
    halve_again = jnp.where((col >> 1) == row, 0.5, 0.0).astype(BF16)
    row, col = grid(256, 256)
    turn = jnp.where(col == ((row & 15) * 16 + (row >> 4)), 1.0, 0.0).astype(BF16)

    loads[0].wait()
    loads[1].wait()
    chunks = []
    for kv, ref in enumerate((k, v)):
        whole = ref[...]
        pair_rows = dot(halve, whole, (1, 0)).astype(BF16)
        quad_rows = dot(halve_again, pair_rows, (1, 0)).astype(BF16)
        mean = jnp.sum(whole.astype(F32), axis=0, keepdims=True) * (1.0 / 256)
        chunks += [mean[:, h * HEAD:(h + 1) * HEAD] for h in range(HEADS)]
        for t in range(STEPS):
            pairs[t, kv] = pair_rows[:, t * HEAD:(t + 1) * HEAD]
            quads[t, kv] = quad_rows[:, t * HEAD:(t + 1) * HEAD]
    tiles_in[member] = jnp.concatenate(chunks, axis=0).astype(BF16)

    pl.semaphore_wait(barrier, len(plane) + len(mates) + 2)

    for _, device in plane:
        post(tiles_in.at[member], tiles_in.at[member], S_TILE, plane_recv.at[0], device)

    def send_step(t, carry):
        cols = pl.ds(pl.multiple_of(t * HEAD, HEAD), HEAD)
        post(quads.at[t], quads_in.at[t, 0], S_QUAD, recv.at[R_QUAD, t], sibling)
        for kv, ref in enumerate((k_in, v_in)):
            post(ref.at[pl.ds(LEAF, LEAF), cols], rim.at[t, kv], S_RIM, recv.at[R_RIM, t], following)
            post(ref.at[pl.ds(0, LEAF), cols], rim.at[t, 2 + kv], S_RIM, recv.at[R_RIM, t], previous)
        post(pairs.at[t], pairs_in.at[t], S_PAIR, recv.at[R_PAIR, t], partner)
        return carry

    lax.fori_loop(0, STEPS, send_step, 0)

    arrived(tiles_in.at[pl.ds(0, PLANE - 1)], plane_recv.at[0])
    for part in range(2):
        turned = dot(turn, tiles_in[part * 16:(part + 1) * 16].reshape(256, HEAD), (1, 0)).astype(BF16)
        for t in range(STEPS):
            for kv in range(2):
                first = (kv * 8 + t) * 16
                sums[t, group, kv * 32 + part * 16:kv * 32 + (part + 1) * 16, :] = turned[first:first + 16]

    def send_sums(t, carry):
        for _, device in mates:
            post(sums.at[t, group], sums.at[t, group], S_SUM, recv.at[R_SUM, t], device)
        return carry

    lax.fori_loop(0, STEPS, send_sums, 0)

    def forward(t):
        arrived(quads_in.at[t, 0], recv.at[R_QUAD, t])
        post(quads_in.at[t, 0], quads_in.at[t, 1], S_QFWD, recv.at[R_QFWD, t], partner)

    forward(0)
    loads[2].wait()
    loads[3].wait()

    row, col = grid(256, 256)
    covered = (((row >> 5) & 3) == x) & (((row & 31) >> 1) == z * 2 + ylo)
    row, col = grid(128, 256)
    absent = ((col < LEAF) & (span == 0)) | ((col >= LEAF) & (span == SPANS - 1))

    def columns(t):
        return pl.ds(pl.multiple_of(t * HEAD, HEAD), HEAD)

    def rows_of(t, kv, ref):
        return jnp.concatenate(
            [
                ref[:, columns(t)],
                pairs_in[t, kv],
                quads_in[t, 0, kv],
                quads_in[t, 1, kv],
                sums[t, :, kv * 32:(kv + 1) * 32, :].reshape(SPANS, HEAD),
            ],
            axis=0,
        )

    def send_rims(t):
        two, other_two = pl.ds(0, 2), pl.ds(2, 2)
        post(rgrad.at[t, two], rgrad_in.at[t, other_two], S_RGRAD, recv.at[R_RGRAD, t], previous)
        post(rgrad.at[t, other_two], rgrad_in.at[t, two], S_RGRAD, recv.at[R_RGRAD, t], following)

    def compute(t):
        @pl.when(t + 1 < STEPS)
        def _():
            forward(t + 1)

        arrived(rim.at[t], recv.at[R_RIM, t])
        arrived(pairs_in.at[t], recv.at[R_PAIR, t])
        arrived(quads_in.at[t, 1], recv.at[R_QFWD, t])
        arrived(sums.at[t, pl.ds(0, GROUP - 1)], recv.at[R_SUM, t])
        cols = columns(t)
        qh, ch = q[:, cols], cot[:, cols]

        def against(main, left, right, other):
            at_rim = jnp.concatenate(
                [dot(left, other[:LEAF], (1, 1)), dot(right, other[LEAF:], (1, 1))], axis=1
            )
            return jnp.concatenate([dot(main, other, (1, 1)), at_rim], axis=0)

        keys, values = rows_of(t, 0, k), rows_of(t, 1, v)
        key_l, value_l, key_r, value_r = rim[t, 0], rim[t, 1], rim[t, 2], rim[t, 3]
        scores = against(keys, key_l, key_r, qh)
        scores = jnp.concatenate(
            [
                scores[:512],
                jnp.where(covered, -1e30, scores[512:768]),
                jnp.where(absent, -1e30, scores[768:]),
            ],
            axis=0,
        )
        highest = jnp.max(scores, axis=0, keepdims=True)
        weights = jnp.exp2((scores - highest) * (SCALE * LOG2E))
        probs = weights * (1.0 / jnp.sum(weights, axis=0, keepdims=True))
        probs_low = probs.astype(BF16)
        dprobs = against(values, value_l, value_r, ch)
        centre = jnp.sum(probs * dprobs, axis=0, keepdims=True)
        dscores = (probs * (dprobs - centre)).astype(BF16)

        probs_kept[t] = probs_low
        dscores_kept[t] = dscores

        sides = ((dscores, qh, SCALE), (probs_low, ch, 1.0))
        for kv, (low, other, factor) in enumerate(sides):
            far = (dot(low[512:768], other, (1, 0)) * factor).astype(BF16)
            sgrad[t, :, kv * 32:(kv + 1) * 32, :] = far.reshape(GROUP, 32, HEAD)
        for there, device in mates:
            post(sgrad.at[t, there], sgrad_in.at[t, group], S_SGRAD, recv.at[R_SGRAD, t], device)
        sgrad_in[t, group] = sgrad[t, group]

        for kv, (low, other, factor) in enumerate(sides):
            rgrad[t, kv] = (dot(low[768:, :LEAF], other[:LEAF], (1, 0)) * factor).astype(BF16)
            rgrad[t, 2 + kv] = (dot(low[768:, LEAF:], other[LEAF:], (1, 0)) * factor).astype(BF16)
        @pl.when(t < HOLD)
        def _():
            send_rims(t)

        for kv, (low, other, factor) in enumerate(sides):
            coarse = dot(low[256:512], other, (1, 0)) * factor
            pgrad[t, kv, 0:128, :] = coarse[:128].astype(BF16)
            qkeep[t, kv] = coarse[128:192]
            pgrad[t, kv, 128:192, :] = coarse[192:].astype(BF16)
        post(pgrad.at[t], pgrad_in.at[t], S_PGRAD, recv.at[R_PGRAD, t], partner)

    def gathered(t, kv, ref, weights):
        total = dot(rows_of(t, kv, ref), weights[:768], (0, 0))
        at_rim = jnp.concatenate(
            [
                dot(rim[t, kv], weights[768:, :LEAF], (0, 0)),
                dot(rim[t, 2 + kv], weights[768:, LEAF:], (0, 0)),
            ],
            axis=1,
        )
        return (total + at_rim).T

    def put(t, refs, value):
        each = STEPS // len(refs)
        for i, ref in enumerate(refs):
            @pl.when(lax.div(t, each) == i)
            def _(ref=ref):
                ref[:, columns(lax.rem(t, each))] = value

    def gather(t):
        put(t, (att0, att1), gathered(t, 1, v, probs_kept[t]).astype(BF16))
        put(t, (gq0, gq1, gq2, gq3), gathered(t, 0, k, dscores_kept[t]) * SCALE)

    def halves(t):
        arrived(pgrad_in.at[t], recv.at[R_PGRAD, t])
        qgrad[t] = (qkeep[t] + pgrad_in[t, :, 128:192, :].astype(F32)).astype(BF16)
        post(qgrad.at[t], qgrad_in.at[t], S_QGRAD, recv.at[R_QGRAD, t], sibling)

    def reduce(t):
        arrived(sgrad_in.at[t, pl.ds(0, GROUP - 1)], recv.at[R_SGRAD, t])
        total = jnp.sum(sgrad_in[t].astype(F32), axis=0).astype(BF16)
        for kv in range(2):
            for part in range(2):
                first = kv * 32 + part * 16
                stage[part, kv * 8 + t] = total[first:first + 16]

    row, col = grid(256, 128)
    double = jnp.where((row >> 1) == col, 0.5, 0.0).astype(BF16)
    row, col = grid(256, 64)
    double_twice = jnp.where((row >> 2) == col, 0.25, 0.0).astype(BF16)

    def join(t):
        arrived(rgrad_in.at[t], recv.at[R_RGRAD, t])
        arrived(qgrad_in.at[t], recv.at[R_QGRAD, t])
        cols = columns(t)
        sides = ((dscores_kept, q, (gk0, gk1, gk2, gk3), SCALE), (probs_kept, cot, (gv0, gv1, gv2, gv3), 1.0))
        for kv, (low, other, out, factor) in enumerate(sides):
            own = dot(low[t, 0:256, :], other[:, cols], (1, 0)) * factor
            ends = jnp.concatenate([rgrad_in[t, kv], rgrad_in[t, 2 + kv]], axis=0).astype(F32)
            coarse = dot(double, pgrad_in[t, kv, 0:128, :], (1, 0)) + dot(double_twice, qgrad_in[t, kv], (1, 0))
            put(t, out, own + ends + coarse)

    def step(t, carry):
        compute(t)

        @pl.when(t >= HALF_LAG)
        def _():
            halves(t - HALF_LAG)

        @pl.when(t >= POST_LAG)
        def _():
            reduce(t - POST_LAG)

        return carry

    def repeat(f):
        def body(t, carry):
            f(t)
            return carry

        return body

    lax.fori_loop(0, STEPS, step, 0)
    lax.fori_loop(STEPS - HALF_LAG, STEPS, repeat(halves), 0)
    lax.fori_loop(STEPS - POST_LAG, STEPS, repeat(reduce), 0)

    for part in range(2):
        turned = dot(turn, stage[part].reshape(256, HEAD), (1, 0)).astype(BF16)
        back[part * 16:(part + 1) * 16] = turned.reshape(16, 16, HEAD)
    for there, device in plane:
        post(back.at[there], back_in.at[member], S_BACK, plane_recv.at[1], device)
    back_in[member] = back[member]
    lax.fori_loop(HOLD, STEPS, repeat(send_rims), 0)

    lax.fori_loop(0, STEPS, repeat(gather), 0)
    lax.fori_loop(0, STEPS, repeat(join), 0)
    arrived(back_in.at[pl.ds(0, PLANE - 1)], plane_recv.at[1])
    total = jnp.sum(back_in[...].astype(F32), axis=0)
    for c in range(2 * HEADS):
        sg[:, c * HEAD:(c + 1) * HEAD] = total[c:c + 1]

    arrived(tiles_in.at[pl.ds(0, PLANE - 1)], send.at[S_TILE])
    arrived(rim, send.at[S_RIM])
    arrived(pairs, send.at[S_PAIR])
    arrived(quads, send.at[S_QUAD])
    arrived(quads, send.at[S_QFWD])
    arrived(sums.at[:, pl.ds(0, GROUP - 1)], send.at[S_SUM])
    arrived(rgrad, send.at[S_RGRAD])
    arrived(pgrad, send.at[S_PGRAD])
    arrived(qgrad, send.at[S_QGRAD])
    arrived(sgrad.at[:, pl.ds(0, GROUP - 1)], send.at[S_SGRAD])
    arrived(back.at[pl.ds(0, PLANE - 1)], send.at[S_BACK])


def finish(*refs):
    pieces, sg, outs, (kept, sem) = refs[:14], refs[14], refs[15:20], refs[20:]
    copies = [pltpu.make_async_copy(sg, outs[4], sem.at[14])]
    copies[0].start()
    for i, piece in enumerate(pieces):
        out, at = (outs[0], i) if i < 2 else (outs[1 + (i - 2) // 4], (i - 2) % 4)
        width = piece.shape[1]
        if i >= 6:
            kept[i - 6] = piece[...] + sg[:, (i - 6) * width:(i - 5) * width] * (1.0 / 256)
            piece = kept.at[i - 6]
        copies.append(pltpu.make_async_copy(piece, out.at[:, pl.ds(at * width, width)], sem.at[i]))
        copies[-1].start()
    for copy in copies:
        copy.wait()


def on_device(queries, keys, values, cotangent):
    rows, width = queries.shape
    in_vmem = pl.BlockSpec(memory_space=pltpu.VMEM)
    in_hbm = pl.BlockSpec(memory_space=pltpu.HBM)
    out_shape = (
        jax.ShapeDtypeStruct((rows, width), BF16),
        jax.ShapeDtypeStruct((rows, width), F32),
        jax.ShapeDtypeStruct((rows, width), F32),
        jax.ShapeDtypeStruct((rows, width), F32),
        jax.ShapeDtypeStruct((1, 2 * width), F32),
    )
    pieces = (
        [jax.ShapeDtypeStruct((rows, width // 2), BF16)] * 2
        + [jax.ShapeDtypeStruct((rows, width // 4), F32)] * 12
        + [jax.ShapeDtypeStruct((1, 2 * width), F32)]
    )
    block = (STEPS, 4, LEAF, HEAD)
    parts = pl.pallas_call(
        kernel,
        out_shape=pieces,
        in_specs=[in_hbm] * 4,
        out_specs=[in_vmem] * 15,
        scratch_shapes=[pltpu.VMEM((rows, width), BF16)] * 4 + [
            pltpu.VMEM((PLANE, 16, HEAD), BF16),
            pltpu.VMEM((STEPS, GROUP, 64, HEAD), BF16),
            pltpu.VMEM(block, BF16),
            pltpu.VMEM((STEPS, 2, 128, HEAD), BF16),
            pltpu.VMEM((STEPS, 2, 128, HEAD), BF16),
            pltpu.VMEM((STEPS, 2, 64, HEAD), BF16),
            pltpu.VMEM((STEPS, 2, 2, 64, HEAD), BF16),
            pltpu.VMEM(block, BF16),
            pltpu.VMEM(block, BF16),
            pltpu.VMEM((STEPS, 2, 192, HEAD), BF16),
            pltpu.VMEM((STEPS, 2, 192, HEAD), BF16),
            pltpu.VMEM((STEPS, 2, 64, HEAD), F32),
            pltpu.VMEM((STEPS, 2, 64, HEAD), BF16),
            pltpu.VMEM((STEPS, 2, 64, HEAD), BF16),
            pltpu.VMEM((STEPS, GROUP, 64, HEAD), BF16),
            pltpu.VMEM((STEPS, GROUP, 64, HEAD), BF16),
            pltpu.VMEM((STEPS, 896, 256), BF16),
            pltpu.VMEM((STEPS, 896, 256), BF16),
            pltpu.VMEM((2, 16, 16, HEAD), BF16),
            pltpu.VMEM((PLANE, 16, HEAD), BF16),
            pltpu.VMEM((PLANE, 16, HEAD), BF16),
            pltpu.SemaphoreType.DMA((11,)),
            pltpu.SemaphoreType.DMA((9, STEPS)),
            pltpu.SemaphoreType.DMA((2,)),
            pltpu.SemaphoreType.DMA((4,)),
        ],
        compiler_params=pltpu.CompilerParams(
            collective_id=0, has_side_effects=True, vmem_limit_bytes=50 * 2**20
        ),
        name="attend",
    )(queries, keys, values, cotangent)
    return pl.pallas_call(
        finish,
        out_shape=out_shape,
        in_specs=[in_vmem] * 15,
        out_specs=(in_hbm,) * 5,
        scratch_shapes=[
            pltpu.VMEM((8, rows, width // 4), F32),
            pltpu.SemaphoreType.DMA((15,)),
        ],
        compiler_params=pltpu.CompilerParams(vmem_limit_bytes=16 * 2**20),
        name="finish",
    )(*parts)


def solution(mesh):
    spec = P(("seq", "outer"), None)
    return jax.shard_map(
        on_device, mesh=mesh, in_specs=(spec,) * 4, out_specs=(spec,) * 5, check_vma=False
    )
```

```python
import functools

import jax
import jax.numpy as jnp
from jax import lax
from jax.experimental import pallas as pl
from jax.experimental.pallas import tpu as pltpu
from jax.sharding import PartitionSpec as P

HEADS = 8
HEAD = 128
LEAF = 128
SPANS = 256
STEPS = 8
PLANE = 32
ZS, YS, XS = 8, 4, 4
GROUP = 2 * XS
WINDOW = 3
HOLD = 4
HALF_LAG = 2
POST_LAG = 5
SCALE = HEAD**-0.5
LOG2E = 1.4426950408889634
MESH = pl.DeviceIdType.MESH
BF16 = jnp.bfloat16
F32 = jnp.float32

(
    S_TILE, S_RIM, S_PAIR, S_QUAD, S_QFWD, S_SUM, S_SFWD,
    S_RGRAD, S_PGRAD, S_QGRAD, S_HALF, S_XGRAD, S_BACK,
) = range(13)
R_RIM, R_PAIR, R_QUAD, R_QFWD, R_SUM, R_SFWD, R_RGRAD, R_PGRAD, R_QGRAD, R_HALF, R_XGRAD = range(11)


def dot(a, b, contract):
    return lax.dot_general(a, b, ((contract[:1], contract[1:]), ((), ())), preferred_element_type=F32)


def kernel(
    q_in, k_in, v_in, cot_in,
    att0, att1, gq0, gq1, gq2, gq3, gk0, gk1, gk2, gk3, gv0, gv1, gv2, gv3, sg,
    q, k, v, cot,
    tiles_in, sums, rim, pairs, pairs_in, quads, quads_in,
    rgrad, rgrad_in, pgrad, pgrad_in, qkeep, qgrad, qgrad_in,
    sgrad, half_in, xgrad, xgrad_in, probs_kept, dscores_kept, stage, back, back_in,
    send, recv, plane_recv, load,
):
    seq, outer = lax.axis_index("seq"), lax.axis_index("outer")
    x, ylo, z = lax.div(seq, 16), lax.rem(lax.div(seq, 8), 2), lax.rem(seq, 8)
    yhi, core = lax.div(outer, 2), lax.rem(outer, 2)
    span = seq * 4 + outer
    y = ylo * 2 + yhi
    member = z * 4 + y

    def at(x, y, z):
        return ((x * 2 + lax.div(y, 2)) * 8 + z, lax.rem(y, 2) * 2 + core)

    def of_span(s):
        return (lax.div(s, 4), lax.rem(s, 4))

    following = of_span(lax.rem(span + 1, SPANS))
    previous = of_span(lax.rem(span + SPANS - 1, SPANS))
    partner = (seq, yhi * 2 + 1 - core)
    sibling = (seq, (1 - yhi) * 2 + core)
    plane = [
        (lax.rem(z + dz, ZS) * YS + lax.rem(y + dy, YS), at(x, lax.rem(y + dy, YS), lax.rem(z + dz, ZS)))
        for dz in (4, 3, 5, 2, 6, 1, 7, 0)
        for dy in (2, 1, 3, 0)
        if dz or dy
    ]
    group = core * XS + x
    mates = [
        (there, ((there * 2 + ylo) * 8 + z, outer)) for there in (lax.rem(x + d, XS) for d in (2, 1, 3))
    ]

    loads = [
        pltpu.make_async_copy(src, dst, load.at[i])
        for i, (src, dst) in enumerate(((k_in, k), (v_in, v), (q_in, q), (cot_in, cot)))
    ]
    for copy in loads:
        copy.start()

    def post(src, dst, s, r, device):
        pltpu.make_async_remote_copy(
            src_ref=src, dst_ref=dst, send_sem=send.at[s], recv_sem=r, device_id=device, device_id_type=MESH
        ).start()

    def arrived(ref, sem):
        pltpu.make_async_copy(ref, ref, sem).wait()

    barrier = pltpu.get_barrier_semaphore()

    def greet(device):
        pl.semaphore_signal(barrier, inc=1, device_id=device, device_id_type=MESH)

    for _, device in plane + mates:
        greet(device)
    greet(partner)
    greet(following)
    greet(previous)

    def grid(rows, cols):
        return (
            lax.broadcasted_iota(jnp.int32, (rows, cols), 0),
            lax.broadcasted_iota(jnp.int32, (rows, cols), 1),
        )

    row, col = grid(128, 256)
    halve = jnp.where((col >> 1) == row, 0.5, 0.0).astype(BF16)
    row, col = grid(64, 128)
    halve_again = jnp.where((col >> 1) == row, 0.5, 0.0).astype(BF16)
    row, col = grid(256, 256)
    turn = jnp.where(col == ((row & 15) * 16 + (row >> 4)), 1.0, 0.0).astype(BF16)

    loads[0].wait()
    loads[1].wait()
    chunks = []
    for kv, ref in enumerate((k, v)):
        whole = ref[...]
        pair_rows = dot(halve, whole, (1, 0)).astype(BF16)
        quad_rows = dot(halve_again, pair_rows, (1, 0)).astype(BF16)
        mean = jnp.sum(whole.astype(F32), axis=0, keepdims=True) * (1.0 / 256)
        chunks += [mean[:, h * HEAD:(h + 1) * HEAD] for h in range(HEADS)]
        for t in range(STEPS):
            pairs[t, kv] = pair_rows[:, t * HEAD:(t + 1) * HEAD]
            quads[t, kv] = quad_rows[:, t * HEAD:(t + 1) * HEAD]
    tiles_in[member] = jnp.concatenate(chunks, axis=0).astype(BF16)

    pl.semaphore_wait(barrier, len(plane) + len(mates) + 3)

    for _, device in plane:
        post(tiles_in.at[member], tiles_in.at[member], S_TILE, plane_recv.at[0], device)

    def send_step(t, carry):
        cols = pl.ds(pl.multiple_of(t * HEAD, HEAD), HEAD)
        post(quads.at[t], quads_in.at[t, 0], S_QUAD, recv.at[R_QUAD, t], sibling)
        for kv, ref in enumerate((k_in, v_in)):
            post(ref.at[pl.ds(LEAF, LEAF), cols], rim.at[t, kv], S_RIM, recv.at[R_RIM, t], following)
            post(ref.at[pl.ds(0, LEAF), cols], rim.at[t, 2 + kv], S_RIM, recv.at[R_RIM, t], previous)
        post(pairs.at[t], pairs_in.at[t], S_PAIR, recv.at[R_PAIR, t], partner)
        return carry

    lax.fori_loop(0, STEPS, send_step, 0)

    arrived(tiles_in.at[pl.ds(0, PLANE - 1)], plane_recv.at[0])
    for part in range(2):
        turned = dot(turn, tiles_in[part * 16:(part + 1) * 16].reshape(256, HEAD), (1, 0)).astype(BF16)
        for t in range(STEPS):
            for kv in range(2):
                first = (kv * 8 + t) * 16
                sums[t, group, kv * 32 + part * 16:kv * 32 + (part + 1) * 16, :] = turned[first:first + 16]

    def send_sums(t, carry):
        for _, device in mates:
            post(sums.at[t, group], sums.at[t, group], S_SUM, recv.at[R_SUM, t], device)
        return carry

    lax.fori_loop(0, WINDOW, send_sums, 0)

    def forward(t):
        arrived(quads_in.at[t, 0], recv.at[R_QUAD, t])
        post(quads_in.at[t, 0], quads_in.at[t, 1], S_QFWD, recv.at[R_QFWD, t], partner)
        arrived(sums.at[t, pl.ds(0, XS - 1)], recv.at[R_SUM, t])
        four = sums.at[t, pl.ds(core * XS, XS)]
        post(four, four, S_SFWD, recv.at[R_SFWD, t], partner)

    forward(0)
    loads[2].wait()
    loads[3].wait()

    row, col = grid(256, 256)
    covered = (((row >> 5) & 3) == x) & (((row & 31) >> 1) == z * 2 + ylo)
    row, col = grid(128, 256)
    absent = ((col < LEAF) & (span == 0)) | ((col >= LEAF) & (span == SPANS - 1))

    def columns(t):
        return pl.ds(pl.multiple_of(t * HEAD, HEAD), HEAD)

    def rows_of(t, kv, ref):
        return jnp.concatenate(
            [
                ref[:, columns(t)],
                pairs_in[t, kv],
                quads_in[t, 0, kv],
                quads_in[t, 1, kv],
                sums[t, :, kv * 32:(kv + 1) * 32, :].reshape(SPANS, HEAD),
            ],
            axis=0,
        )

    def send_rims(t):
        two, other_two = pl.ds(0, 2), pl.ds(2, 2)
        post(rgrad.at[t, two], rgrad_in.at[t, other_two], S_RGRAD, recv.at[R_RGRAD, t], previous)
        post(rgrad.at[t, other_two], rgrad_in.at[t, two], S_RGRAD, recv.at[R_RGRAD, t], following)

    def compute(t):
        @pl.when(t + WINDOW < STEPS)
        def _():
            send_sums(t + WINDOW, 0)

        @pl.when(t + 1 < STEPS)
        def _():
            forward(t + 1)

        arrived(rim.at[t], recv.at[R_RIM, t])
        arrived(pairs_in.at[t], recv.at[R_PAIR, t])
        arrived(quads_in.at[t, 1], recv.at[R_QFWD, t])
        arrived(sums.at[t, pl.ds(0, XS)], recv.at[R_SFWD, t])
        cols = columns(t)
        qh, ch = q[:, cols], cot[:, cols]

        def against(main, left, right, other):
            at_rim = jnp.concatenate(
                [dot(left, other[:LEAF], (1, 1)), dot(right, other[LEAF:], (1, 1))], axis=1
            )
            return jnp.concatenate([dot(main, other, (1, 1)), at_rim], axis=0)

        keys, values = rows_of(t, 0, k), rows_of(t, 1, v)
        key_l, value_l, key_r, value_r = rim[t, 0], rim[t, 1], rim[t, 2], rim[t, 3]
        scores = against(keys, key_l, key_r, qh)
        scores = jnp.concatenate(
            [
                scores[:512],
                jnp.where(covered, -1e30, scores[512:768]),
                jnp.where(absent, -1e30, scores[768:]),
            ],
            axis=0,
        )
        highest = jnp.max(scores, axis=0, keepdims=True)
        weights = jnp.exp2((scores - highest) * (SCALE * LOG2E))
        probs = weights * (1.0 / jnp.sum(weights, axis=0, keepdims=True))
        probs_low = probs.astype(BF16)
        dprobs = against(values, value_l, value_r, ch)
        centre = jnp.sum(probs * dprobs, axis=0, keepdims=True)
        dscores = (probs * (dprobs - centre)).astype(BF16)

        probs_kept[t] = probs_low
        dscores_kept[t] = dscores

        sides = ((dscores, qh, SCALE), (probs_low, ch, 1.0))
        for kv, (low, other, factor) in enumerate(sides):
            far = (dot(low[512:768], other, (1, 0)) * factor).astype(BF16)
            sgrad[t, :, kv * 32:(kv + 1) * 32, :] = far.reshape(GROUP, 32, HEAD)
        post(sgrad.at[t, pl.ds((1 - core) * XS, XS)], half_in.at[t], S_HALF, recv.at[R_HALF, t], partner)

        for kv, (low, other, factor) in enumerate(sides):
            rgrad[t, kv] = (dot(low[768:, :LEAF], other[:LEAF], (1, 0)) * factor).astype(BF16)
            rgrad[t, 2 + kv] = (dot(low[768:, LEAF:], other[LEAF:], (1, 0)) * factor).astype(BF16)
        @pl.when(t < HOLD)
        def _():
            send_rims(t)

        for kv, (low, other, factor) in enumerate(sides):
            coarse = dot(low[256:512], other, (1, 0)) * factor
            pgrad[t, kv, 0:128, :] = coarse[:128].astype(BF16)
            qkeep[t, kv] = coarse[128:192]
            pgrad[t, kv, 128:192, :] = coarse[192:].astype(BF16)
        post(pgrad.at[t], pgrad_in.at[t], S_PGRAD, recv.at[R_PGRAD, t], partner)

    def gathered(t, kv, ref, weights):
        total = dot(rows_of(t, kv, ref), weights[:768], (0, 0))
        at_rim = jnp.concatenate(
            [
                dot(rim[t, kv], weights[768:, :LEAF], (0, 0)),
                dot(rim[t, 2 + kv], weights[768:, LEAF:], (0, 0)),
            ],
            axis=1,
        )
        return (total + at_rim).T

    def put(t, refs, value):
        each = STEPS // len(refs)
        for i, ref in enumerate(refs):
            @pl.when(lax.div(t, each) == i)
            def _(ref=ref):
                ref[:, columns(lax.rem(t, each))] = value

    def gather(t):
        put(t, (att0, att1), gathered(t, 1, v, probs_kept[t]).astype(BF16))
        put(t, (gq0, gq1, gq2, gq3), gathered(t, 0, k, dscores_kept[t]) * SCALE)

    def halves(t):
        arrived(half_in.at[t], recv.at[R_HALF, t])
        own = sgrad[t, pl.ds(core * XS, XS)].astype(F32)
        xgrad[t] = (own + half_in[t].astype(F32)).astype(BF16)
        for there, device in mates:
            post(xgrad.at[t, there], xgrad_in.at[t, x], S_XGRAD, recv.at[R_XGRAD, t], device)
        xgrad_in[t, x] = xgrad[t, x]
        arrived(pgrad_in.at[t], recv.at[R_PGRAD, t])
        qgrad[t] = (qkeep[t] + pgrad_in[t, :, 128:192, :].astype(F32)).astype(BF16)
        post(qgrad.at[t], qgrad_in.at[t], S_QGRAD, recv.at[R_QGRAD, t], sibling)

    def reduce(t):
        arrived(xgrad_in.at[t, pl.ds(0, XS - 1)], recv.at[R_XGRAD, t])
        total = jnp.sum(xgrad_in[t].astype(F32), axis=0).astype(BF16)
        for kv in range(2):
            for part in range(2):
                first = kv * 32 + part * 16
                stage[part, kv * 8 + t] = total[first:first + 16]

    row, col = grid(256, 128)
    double = jnp.where((row >> 1) == col, 0.5, 0.0).astype(BF16)
    row, col = grid(256, 64)
    double_twice = jnp.where((row >> 2) == col, 0.25, 0.0).astype(BF16)

    def join(t):
        arrived(rgrad_in.at[t], recv.at[R_RGRAD, t])
        arrived(qgrad_in.at[t], recv.at[R_QGRAD, t])
        cols = columns(t)
        sides = ((dscores_kept, q, (gk0, gk1, gk2, gk3), SCALE), (probs_kept, cot, (gv0, gv1, gv2, gv3), 1.0))
        for kv, (low, other, out, factor) in enumerate(sides):
            own = dot(low[t, 0:256, :], other[:, cols], (1, 0)) * factor
            ends = jnp.concatenate([rgrad_in[t, kv], rgrad_in[t, 2 + kv]], axis=0).astype(F32)
            coarse = dot(double, pgrad_in[t, kv, 0:128, :], (1, 0)) + dot(double_twice, qgrad_in[t, kv], (1, 0))
            put(t, out, own + ends + coarse)

    def step(t, carry):
        compute(t)

        @pl.when(t >= HALF_LAG)
        def _():
            halves(t - HALF_LAG)

        @pl.when(t >= POST_LAG)
        def _():
            reduce(t - POST_LAG)

        return carry

    def repeat(f):
        def body(t, carry):
            f(t)
            return carry

        return body

    lax.fori_loop(0, STEPS, step, 0)
    lax.fori_loop(STEPS - HALF_LAG, STEPS, repeat(halves), 0)
    lax.fori_loop(STEPS - POST_LAG, STEPS, repeat(reduce), 0)

    for part in range(2):
        turned = dot(turn, stage[part].reshape(256, HEAD), (1, 0)).astype(BF16)
        back[part * 16:(part + 1) * 16] = turned.reshape(16, 16, HEAD)
    for there, device in plane:
        post(back.at[there], back_in.at[member], S_BACK, plane_recv.at[1], device)
    back_in[member] = back[member]
    lax.fori_loop(HOLD, STEPS, repeat(send_rims), 0)

    lax.fori_loop(0, STEPS, repeat(gather), 0)
    lax.fori_loop(0, STEPS, repeat(join), 0)
    arrived(back_in.at[pl.ds(0, PLANE - 1)], plane_recv.at[1])
    total = jnp.sum(back_in[...].astype(F32), axis=0)
    for c in range(2 * HEADS):
        sg[:, c * HEAD:(c + 1) * HEAD] = total[c:c + 1]

    arrived(tiles_in.at[pl.ds(0, PLANE - 1)], send.at[S_TILE])
    arrived(rim, send.at[S_RIM])
    arrived(pairs, send.at[S_PAIR])
    arrived(quads, send.at[S_QUAD])
    arrived(quads, send.at[S_QFWD])
    arrived(sums.at[:, pl.ds(0, XS - 1)], send.at[S_SUM])
    arrived(sums.at[:, pl.ds(0, XS)], send.at[S_SFWD])
    arrived(rgrad, send.at[S_RGRAD])
    arrived(pgrad, send.at[S_PGRAD])
    arrived(qgrad, send.at[S_QGRAD])
    arrived(half_in, send.at[S_HALF])
    arrived(xgrad.at[:, pl.ds(0, XS - 1)], send.at[S_XGRAD])
    arrived(back.at[pl.ds(0, PLANE - 1)], send.at[S_BACK])


def finish(*refs):
    pieces, sg, outs, (kept, sem) = refs[:14], refs[14], refs[15:20], refs[20:]
    copies = [pltpu.make_async_copy(sg, outs[4], sem.at[14])]
    copies[0].start()
    for i, piece in enumerate(pieces):
        out, at = (outs[0], i) if i < 2 else (outs[1 + (i - 2) // 4], (i - 2) % 4)
        width = piece.shape[1]
        if i >= 6:
            kept[i - 6] = piece[...] + sg[:, (i - 6) * width:(i - 5) * width] * (1.0 / 256)
            piece = kept.at[i - 6]
        copies.append(pltpu.make_async_copy(piece, out.at[:, pl.ds(at * width, width)], sem.at[i]))
        copies[-1].start()
    for copy in copies:
        copy.wait()


def on_device(queries, keys, values, cotangent):
    rows, width = queries.shape
    in_vmem = pl.BlockSpec(memory_space=pltpu.VMEM)
    in_hbm = pl.BlockSpec(memory_space=pltpu.HBM)
    out_shape = (
        jax.ShapeDtypeStruct((rows, width), BF16),
        jax.ShapeDtypeStruct((rows, width), F32),
        jax.ShapeDtypeStruct((rows, width), F32),
        jax.ShapeDtypeStruct((rows, width), F32),
        jax.ShapeDtypeStruct((1, 2 * width), F32),
    )
    pieces = (
        [jax.ShapeDtypeStruct((rows, width // 2), BF16)] * 2
        + [jax.ShapeDtypeStruct((rows, width // 4), F32)] * 12
        + [jax.ShapeDtypeStruct((1, 2 * width), F32)]
    )
    block = (STEPS, 4, LEAF, HEAD)
    parts = pl.pallas_call(
        kernel,
        out_shape=pieces,
        in_specs=[in_hbm] * 4,
        out_specs=[in_vmem] * 15,
        scratch_shapes=[pltpu.VMEM((rows, width), BF16)] * 4 + [
            pltpu.VMEM((PLANE, 16, HEAD), BF16),
            pltpu.VMEM((STEPS, GROUP, 64, HEAD), BF16),
            pltpu.VMEM(block, BF16),
            pltpu.VMEM((STEPS, 2, 128, HEAD), BF16),
            pltpu.VMEM((STEPS, 2, 128, HEAD), BF16),
            pltpu.VMEM((STEPS, 2, 64, HEAD), BF16),
            pltpu.VMEM((STEPS, 2, 2, 64, HEAD), BF16),
            pltpu.VMEM(block, BF16),
            pltpu.VMEM(block, BF16),
            pltpu.VMEM((STEPS, 2, 192, HEAD), BF16),
            pltpu.VMEM((STEPS, 2, 192, HEAD), BF16),
            pltpu.VMEM((STEPS, 2, 64, HEAD), F32),
            pltpu.VMEM((STEPS, 2, 64, HEAD), BF16),
            pltpu.VMEM((STEPS, 2, 64, HEAD), BF16),
            pltpu.VMEM((STEPS, GROUP, 64, HEAD), BF16),
            pltpu.VMEM((STEPS, XS, 64, HEAD), BF16),
            pltpu.VMEM((STEPS, XS, 64, HEAD), BF16),
            pltpu.VMEM((STEPS, XS, 64, HEAD), BF16),
            pltpu.VMEM((STEPS, 896, 256), BF16),
            pltpu.VMEM((STEPS, 896, 256), BF16),
            pltpu.VMEM((2, 16, 16, HEAD), BF16),
            pltpu.VMEM((PLANE, 16, HEAD), BF16),
            pltpu.VMEM((PLANE, 16, HEAD), BF16),
            pltpu.SemaphoreType.DMA((13,)),
            pltpu.SemaphoreType.DMA((11, STEPS)),
            pltpu.SemaphoreType.DMA((2,)),
            pltpu.SemaphoreType.DMA((4,)),
        ],
        compiler_params=pltpu.CompilerParams(
            collective_id=0, has_side_effects=True, vmem_limit_bytes=50 * 2**20
        ),
        name="attend",
    )(queries, keys, values, cotangent)
    return pl.pallas_call(
        finish,
        out_shape=out_shape,
        in_specs=[in_vmem] * 15,
        out_specs=(in_hbm,) * 5,
        scratch_shapes=[
            pltpu.VMEM((8, rows, width // 4), F32),
            pltpu.SemaphoreType.DMA((15,)),
        ],
        compiler_params=pltpu.CompilerParams(vmem_limit_bytes=16 * 2**20),
        name="finish",
    )(*parts)


def solution(mesh):
    spec = P(("seq", "outer"), None)
    return jax.shard_map(
        on_device, mesh=mesh, in_specs=(spec,) * 4, out_specs=(spec,) * 5, check_vma=False
    )
```

```python
import functools

import jax
import jax.numpy as jnp
from jax import lax
from jax.experimental import pallas as pl
from jax.experimental.pallas import tpu as pltpu
from jax.sharding import PartitionSpec as P

HEADS = 8
HEAD = 128
LEAF = 128
SPANS = 256
STEPS = 8
PLANE = 32
ZS, YS, XS = 8, 4, 4
GROUP = 2 * XS
AHEAD = 2
WINDOW = 5
HOLD = 4
HALF_LAG = 2
POST_LAG = 5
SCALE = HEAD**-0.5
LOG2E = 1.4426950408889634
MESH = pl.DeviceIdType.MESH
BF16 = jnp.bfloat16
F32 = jnp.float32

(
    S_TILE, S_RIM, S_PAIR, S_QUAD, S_QFWD, S_SUM, S_SFWD,
    S_RGRAD, S_PGRAD, S_QGRAD, S_HALF, S_XGRAD, S_BACK,
) = range(13)
R_RIM, R_PAIR, R_QUAD, R_QFWD, R_SUM, R_SFWD, R_RGRAD, R_PGRAD, R_QGRAD, R_HALF, R_XGRAD = range(11)


def dot(a, b, contract):
    return lax.dot_general(a, b, ((contract[:1], contract[1:]), ((), ())), preferred_element_type=F32)


def kernel(
    q_in, k_in, v_in, cot_in,
    att0, att1, gq0, gq1, gq2, gq3, gk0, gk1, gk2, gk3, gv0, gv1, gv2, gv3, sg,
    q, k, v, cot,
    tiles_in, sums, rim, pairs, pairs_in, quads, quads_in,
    rgrad, rgrad_in, pgrad, pgrad_in, qkeep, qgrad, qgrad_in,
    sgrad, half_in, xgrad, xgrad_in, probs_kept, dscores_kept, stage, back, back_in,
    send, recv, plane_recv, load,
):
    seq, outer = lax.axis_index("seq"), lax.axis_index("outer")
    x, ylo, z = lax.div(seq, 16), lax.rem(lax.div(seq, 8), 2), lax.rem(seq, 8)
    yhi, core = lax.div(outer, 2), lax.rem(outer, 2)
    span = seq * 4 + outer
    y = ylo * 2 + yhi
    member = z * 4 + y

    def at(x, y, z):
        return ((x * 2 + lax.div(y, 2)) * 8 + z, lax.rem(y, 2) * 2 + core)

    def of_span(s):
        return (lax.div(s, 4), lax.rem(s, 4))

    following = of_span(lax.rem(span + 1, SPANS))
    previous = of_span(lax.rem(span + SPANS - 1, SPANS))
    partner = (seq, yhi * 2 + 1 - core)
    sibling = (seq, (1 - yhi) * 2 + core)
    plane = [
        (lax.rem(z + dz, ZS) * YS + lax.rem(y + dy, YS), at(x, lax.rem(y + dy, YS), lax.rem(z + dz, ZS)))
        for dz in (4, 3, 5, 2, 6, 1, 7, 0)
        for dy in (2, 1, 3, 0)
        if dz or dy
    ]
    group = core * XS + x
    mates = [
        (there, ((there * 2 + ylo) * 8 + z, outer)) for there in (lax.rem(x + d, XS) for d in (2, 1, 3))
    ]

    loads = [
        pltpu.make_async_copy(src, dst, load.at[i])
        for i, (src, dst) in enumerate(((k_in, k), (v_in, v), (q_in, q), (cot_in, cot)))
    ]
    for copy in loads:
        copy.start()

    def post(src, dst, s, r, device):
        pltpu.make_async_remote_copy(
            src_ref=src, dst_ref=dst, send_sem=send.at[s], recv_sem=r, device_id=device, device_id_type=MESH
        ).start()

    def arrived(ref, sem):
        pltpu.make_async_copy(ref, ref, sem).wait()

    barrier = pltpu.get_barrier_semaphore()

    def greet(device):
        pl.semaphore_signal(barrier, inc=1, device_id=device, device_id_type=MESH)

    for _, device in plane + mates:
        greet(device)
    greet(partner)
    greet(following)
    greet(previous)

    def grid(rows, cols):
        return (
            lax.broadcasted_iota(jnp.int32, (rows, cols), 0),
            lax.broadcasted_iota(jnp.int32, (rows, cols), 1),
        )

    row, col = grid(128, 256)
    halve = jnp.where((col >> 1) == row, 0.5, 0.0).astype(BF16)
    row, col = grid(64, 128)
    halve_again = jnp.where((col >> 1) == row, 0.5, 0.0).astype(BF16)
    row, col = grid(256, 256)
    turn = jnp.where(col == ((row & 15) * 16 + (row >> 4)), 1.0, 0.0).astype(BF16)

    loads[0].wait()
    loads[1].wait()
    chunks = []
    for kv, ref in enumerate((k, v)):
        whole = ref[...]
        pair_rows = dot(halve, whole, (1, 0)).astype(BF16)
        quad_rows = dot(halve_again, pair_rows, (1, 0)).astype(BF16)
        mean = jnp.sum(whole.astype(F32), axis=0, keepdims=True) * (1.0 / 256)
        chunks += [mean[:, h * HEAD:(h + 1) * HEAD] for h in range(HEADS)]
        for t in range(STEPS):
            pairs[t, kv] = pair_rows[:, t * HEAD:(t + 1) * HEAD]
            quads[t, kv] = quad_rows[:, t * HEAD:(t + 1) * HEAD]
    tiles_in[member] = jnp.concatenate(chunks, axis=0).astype(BF16)

    pl.semaphore_wait(barrier, len(plane) + len(mates) + 3)

    for _, device in plane:
        post(tiles_in.at[member], tiles_in.at[member], S_TILE, plane_recv.at[0], device)

    def send_step(t, carry):
        cols = pl.ds(pl.multiple_of(t * HEAD, HEAD), HEAD)
        post(quads.at[t], quads_in.at[t, 0], S_QUAD, recv.at[R_QUAD, t], sibling)
        for kv, ref in enumerate((k_in, v_in)):
            post(ref.at[pl.ds(LEAF, LEAF), cols], rim.at[t, kv], S_RIM, recv.at[R_RIM, t], following)
            post(ref.at[pl.ds(0, LEAF), cols], rim.at[t, 2 + kv], S_RIM, recv.at[R_RIM, t], previous)
        post(pairs.at[t], pairs_in.at[t], S_PAIR, recv.at[R_PAIR, t], partner)
        return carry

    lax.fori_loop(0, STEPS, send_step, 0)

    arrived(tiles_in.at[pl.ds(0, PLANE - 1)], plane_recv.at[0])
    for part in range(2):
        turned = dot(turn, tiles_in[part * 16:(part + 1) * 16].reshape(256, HEAD), (1, 0)).astype(BF16)
        for t in range(STEPS):
            for kv in range(2):
                first = (kv * 8 + t) * 16
                sums[t, group, kv * 32 + part * 16:kv * 32 + (part + 1) * 16, :] = turned[first:first + 16]

    def send_sums(t, carry):
        for _, device in mates:
            post(sums.at[t, group], sums.at[t, group], S_SUM, recv.at[R_SUM, t], device)
        return carry

    lax.fori_loop(0, WINDOW, send_sums, 0)

    def forward(t):
        arrived(quads_in.at[t, 0], recv.at[R_QUAD, t])
        post(quads_in.at[t, 0], quads_in.at[t, 1], S_QFWD, recv.at[R_QFWD, t], partner)
        arrived(sums.at[t, pl.ds(0, XS - 1)], recv.at[R_SUM, t])
        four = sums.at[t, pl.ds(core * XS, XS)]
        post(four, four, S_SFWD, recv.at[R_SFWD, t], partner)

    for t in range(AHEAD):
        forward(t)
    loads[2].wait()
    loads[3].wait()

    row, col = grid(256, 256)
    covered = (((row >> 5) & 3) == x) & (((row & 31) >> 1) == z * 2 + ylo)
    row, col = grid(128, 256)
    absent = ((col < LEAF) & (span == 0)) | ((col >= LEAF) & (span == SPANS - 1))

    def columns(t):
        return pl.ds(pl.multiple_of(t * HEAD, HEAD), HEAD)

    def rows_of(t, kv, ref):
        return jnp.concatenate(
            [
                ref[:, columns(t)],
                pairs_in[t, kv],
                quads_in[t, 0, kv],
                quads_in[t, 1, kv],
                sums[t, :, kv * 32:(kv + 1) * 32, :].reshape(SPANS, HEAD),
            ],
            axis=0,
        )

    def send_rims(t):
        two, other_two = pl.ds(0, 2), pl.ds(2, 2)
        post(rgrad.at[t, two], rgrad_in.at[t, other_two], S_RGRAD, recv.at[R_RGRAD, t], previous)
        post(rgrad.at[t, other_two], rgrad_in.at[t, two], S_RGRAD, recv.at[R_RGRAD, t], following)

    def compute(t):
        @pl.when(t + WINDOW < STEPS)
        def _():
            send_sums(t + WINDOW, 0)

        @pl.when(t + AHEAD < STEPS)
        def _():
            forward(t + AHEAD)

        arrived(rim.at[t], recv.at[R_RIM, t])
        arrived(pairs_in.at[t], recv.at[R_PAIR, t])
        arrived(quads_in.at[t, 1], recv.at[R_QFWD, t])
        arrived(sums.at[t, pl.ds(0, XS)], recv.at[R_SFWD, t])
        cols = columns(t)
        qh, ch = q[:, cols], cot[:, cols]

        def against(main, left, right, other):
            at_rim = jnp.concatenate(
                [dot(left, other[:LEAF], (1, 1)), dot(right, other[LEAF:], (1, 1))], axis=1
            )
            return jnp.concatenate([dot(main, other, (1, 1)), at_rim], axis=0)

        keys, values = rows_of(t, 0, k), rows_of(t, 1, v)
        key_l, value_l, key_r, value_r = rim[t, 0], rim[t, 1], rim[t, 2], rim[t, 3]
        scores = against(keys, key_l, key_r, qh)
        scores = jnp.concatenate(
            [
                scores[:512],
                jnp.where(covered, -1e30, scores[512:768]),
                jnp.where(absent, -1e30, scores[768:]),
            ],
            axis=0,
        )
        highest = jnp.max(scores, axis=0, keepdims=True)
        weights = jnp.exp2((scores - highest) * (SCALE * LOG2E))
        probs = weights * (1.0 / jnp.sum(weights, axis=0, keepdims=True))
        probs_low = probs.astype(BF16)
        dprobs = against(values, value_l, value_r, ch)
        centre = jnp.sum(probs * dprobs, axis=0, keepdims=True)
        dscores = (probs * (dprobs - centre)).astype(BF16)

        probs_kept[t] = probs_low
        dscores_kept[t] = dscores

        sides = ((dscores, qh, SCALE), (probs_low, ch, 1.0))
        for kv, (low, other, factor) in enumerate(sides):
            far = (dot(low[512:768], other, (1, 0)) * factor).astype(BF16)
            sgrad[t, :, kv * 32:(kv + 1) * 32, :] = far.reshape(GROUP, 32, HEAD)
        post(sgrad.at[t, pl.ds((1 - core) * XS, XS)], half_in.at[t], S_HALF, recv.at[R_HALF, t], partner)

        for kv, (low, other, factor) in enumerate(sides):
            rgrad[t, kv] = (dot(low[768:, :LEAF], other[:LEAF], (1, 0)) * factor).astype(BF16)
            rgrad[t, 2 + kv] = (dot(low[768:, LEAF:], other[LEAF:], (1, 0)) * factor).astype(BF16)
        @pl.when(t < HOLD)
        def _():
            send_rims(t)

        for kv, (low, other, factor) in enumerate(sides):
            coarse = dot(low[256:512], other, (1, 0)) * factor
            pgrad[t, kv, 0:128, :] = coarse[:128].astype(BF16)
            qkeep[t, kv] = coarse[128:192]
            pgrad[t, kv, 128:192, :] = coarse[192:].astype(BF16)
        post(pgrad.at[t], pgrad_in.at[t], S_PGRAD, recv.at[R_PGRAD, t], partner)

    def gathered(t, kv, ref, weights):
        total = dot(rows_of(t, kv, ref), weights[:768], (0, 0))
        at_rim = jnp.concatenate(
            [
                dot(rim[t, kv], weights[768:, :LEAF], (0, 0)),
                dot(rim[t, 2 + kv], weights[768:, LEAF:], (0, 0)),
            ],
            axis=1,
        )
        return (total + at_rim).T

    def put(t, refs, value):
        each = STEPS // len(refs)
        for i, ref in enumerate(refs):
            @pl.when(lax.div(t, each) == i)
            def _(ref=ref):
                ref[:, columns(lax.rem(t, each))] = value

    def gather(t):
        put(t, (att0, att1), gathered(t, 1, v, probs_kept[t]).astype(BF16))
        put(t, (gq0, gq1, gq2, gq3), gathered(t, 0, k, dscores_kept[t]) * SCALE)

    def halves(t):
        arrived(half_in.at[t], recv.at[R_HALF, t])
        own = sgrad[t, pl.ds(core * XS, XS)].astype(F32)
        xgrad[t] = (own + half_in[t].astype(F32)).astype(BF16)
        for there, device in mates:
            post(xgrad.at[t, there], xgrad_in.at[t, x], S_XGRAD, recv.at[R_XGRAD, t], device)
        xgrad_in[t, x] = xgrad[t, x]
        arrived(pgrad_in.at[t], recv.at[R_PGRAD, t])
        qgrad[t] = (qkeep[t] + pgrad_in[t, :, 128:192, :].astype(F32)).astype(BF16)
        post(qgrad.at[t], qgrad_in.at[t], S_QGRAD, recv.at[R_QGRAD, t], sibling)

    def reduce(t):
        arrived(xgrad_in.at[t, pl.ds(0, XS - 1)], recv.at[R_XGRAD, t])
        total = jnp.sum(xgrad_in[t].astype(F32), axis=0).astype(BF16)
        for kv in range(2):
            for part in range(2):
                first = kv * 32 + part * 16
                stage[part, kv * 8 + t] = total[first:first + 16]

    row, col = grid(256, 128)
    double = jnp.where((row >> 1) == col, 0.5, 0.0).astype(BF16)
    row, col = grid(256, 64)
    double_twice = jnp.where((row >> 2) == col, 0.25, 0.0).astype(BF16)

    def join(t):
        arrived(rgrad_in.at[t], recv.at[R_RGRAD, t])
        arrived(qgrad_in.at[t], recv.at[R_QGRAD, t])
        cols = columns(t)
        sides = ((dscores_kept, q, (gk0, gk1, gk2, gk3), SCALE), (probs_kept, cot, (gv0, gv1, gv2, gv3), 1.0))
        for kv, (low, other, out, factor) in enumerate(sides):
            own = dot(low[t, 0:256, :], other[:, cols], (1, 0)) * factor
            ends = jnp.concatenate([rgrad_in[t, kv], rgrad_in[t, 2 + kv]], axis=0).astype(F32)
            coarse = dot(double, pgrad_in[t, kv, 0:128, :], (1, 0)) + dot(double_twice, qgrad_in[t, kv], (1, 0))
            put(t, out, own + ends + coarse)

    def step(t, carry):
        compute(t)

        @pl.when(t >= HALF_LAG)
        def _():
            halves(t - HALF_LAG)

        @pl.when(t >= POST_LAG)
        def _():
            reduce(t - POST_LAG)

        return carry

    def repeat(f):
        def body(t, carry):
            f(t)
            return carry

        return body

    lax.fori_loop(0, STEPS, step, 0)
    lax.fori_loop(STEPS - HALF_LAG, STEPS, repeat(halves), 0)
    lax.fori_loop(STEPS - POST_LAG, STEPS, repeat(reduce), 0)

    for part in range(2):
        turned = dot(turn, stage[part].reshape(256, HEAD), (1, 0)).astype(BF16)
        back[part * 16:(part + 1) * 16] = turned.reshape(16, 16, HEAD)
    for there, device in plane:
        post(back.at[there], back_in.at[member], S_BACK, plane_recv.at[1], device)
    back_in[member] = back[member]
    lax.fori_loop(HOLD, STEPS, repeat(send_rims), 0)

    lax.fori_loop(0, STEPS, repeat(gather), 0)
    lax.fori_loop(0, STEPS, repeat(join), 0)
    arrived(back_in.at[pl.ds(0, PLANE - 1)], plane_recv.at[1])
    total = jnp.sum(back_in[...].astype(F32), axis=0)
    for c in range(2 * HEADS):
        sg[:, c * HEAD:(c + 1) * HEAD] = total[c:c + 1]

    arrived(tiles_in.at[pl.ds(0, PLANE - 1)], send.at[S_TILE])
    arrived(rim, send.at[S_RIM])
    arrived(pairs, send.at[S_PAIR])
    arrived(quads, send.at[S_QUAD])
    arrived(quads, send.at[S_QFWD])
    arrived(sums.at[:, pl.ds(0, XS - 1)], send.at[S_SUM])
    arrived(sums.at[:, pl.ds(0, XS)], send.at[S_SFWD])
    arrived(rgrad, send.at[S_RGRAD])
    arrived(pgrad, send.at[S_PGRAD])
    arrived(qgrad, send.at[S_QGRAD])
    arrived(half_in, send.at[S_HALF])
    arrived(xgrad.at[:, pl.ds(0, XS - 1)], send.at[S_XGRAD])
    arrived(back.at[pl.ds(0, PLANE - 1)], send.at[S_BACK])


def finish(*refs):
    pieces, sg, outs, (kept, sem) = refs[:14], refs[14], refs[15:20], refs[20:]
    copies = [pltpu.make_async_copy(sg, outs[4], sem.at[14])]
    copies[0].start()
    for i, piece in enumerate(pieces):
        out, at = (outs[0], i) if i < 2 else (outs[1 + (i - 2) // 4], (i - 2) % 4)
        width = piece.shape[1]
        if i >= 6:
            kept[i - 6] = piece[...] + sg[:, (i - 6) * width:(i - 5) * width] * (1.0 / 256)
            piece = kept.at[i - 6]
        copies.append(pltpu.make_async_copy(piece, out.at[:, pl.ds(at * width, width)], sem.at[i]))
        copies[-1].start()
    for copy in copies:
        copy.wait()


def on_device(queries, keys, values, cotangent):
    rows, width = queries.shape
    in_vmem = pl.BlockSpec(memory_space=pltpu.VMEM)
    in_hbm = pl.BlockSpec(memory_space=pltpu.HBM)
    out_shape = (
        jax.ShapeDtypeStruct((rows, width), BF16),
        jax.ShapeDtypeStruct((rows, width), F32),
        jax.ShapeDtypeStruct((rows, width), F32),
        jax.ShapeDtypeStruct((rows, width), F32),
        jax.ShapeDtypeStruct((1, 2 * width), F32),
    )
    pieces = (
        [jax.ShapeDtypeStruct((rows, width // 2), BF16)] * 2
        + [jax.ShapeDtypeStruct((rows, width // 4), F32)] * 12
        + [jax.ShapeDtypeStruct((1, 2 * width), F32)]
    )
    block = (STEPS, 4, LEAF, HEAD)
    parts = pl.pallas_call(
        kernel,
        out_shape=pieces,
        in_specs=[in_hbm] * 4,
        out_specs=[in_vmem] * 15,
        scratch_shapes=[pltpu.VMEM((rows, width), BF16)] * 4 + [
            pltpu.VMEM((PLANE, 16, HEAD), BF16),
            pltpu.VMEM((STEPS, GROUP, 64, HEAD), BF16),
            pltpu.VMEM(block, BF16),
            pltpu.VMEM((STEPS, 2, 128, HEAD), BF16),
            pltpu.VMEM((STEPS, 2, 128, HEAD), BF16),
            pltpu.VMEM((STEPS, 2, 64, HEAD), BF16),
            pltpu.VMEM((STEPS, 2, 2, 64, HEAD), BF16),
            pltpu.VMEM(block, BF16),
            pltpu.VMEM(block, BF16),
            pltpu.VMEM((STEPS, 2, 192, HEAD), BF16),
            pltpu.VMEM((STEPS, 2, 192, HEAD), BF16),
            pltpu.VMEM((STEPS, 2, 64, HEAD), F32),
            pltpu.VMEM((STEPS, 2, 64, HEAD), BF16),
            pltpu.VMEM((STEPS, 2, 64, HEAD), BF16),
            pltpu.VMEM((STEPS, GROUP, 64, HEAD), BF16),
            pltpu.VMEM((STEPS, XS, 64, HEAD), BF16),
            pltpu.VMEM((STEPS, XS, 64, HEAD), BF16),
            pltpu.VMEM((STEPS, XS, 64, HEAD), BF16),
            pltpu.VMEM((STEPS, 896, 256), BF16),
            pltpu.VMEM((STEPS, 896, 256), BF16),
            pltpu.VMEM((2, 16, 16, HEAD), BF16),
            pltpu.VMEM((PLANE, 16, HEAD), BF16),
            pltpu.VMEM((PLANE, 16, HEAD), BF16),
            pltpu.SemaphoreType.DMA((13,)),
            pltpu.SemaphoreType.DMA((11, STEPS)),
            pltpu.SemaphoreType.DMA((2,)),
            pltpu.SemaphoreType.DMA((4,)),
        ],
        compiler_params=pltpu.CompilerParams(
            collective_id=0, has_side_effects=True, vmem_limit_bytes=50 * 2**20
        ),
        name="attend",
    )(queries, keys, values, cotangent)
    return pl.pallas_call(
        finish,
        out_shape=out_shape,
        in_specs=[in_vmem] * 15,
        out_specs=(in_hbm,) * 5,
        scratch_shapes=[
            pltpu.VMEM((8, rows, width // 4), F32),
            pltpu.SemaphoreType.DMA((15,)),
        ],
        compiler_params=pltpu.CompilerParams(vmem_limit_bytes=16 * 2**20),
        name="finish",
    )(*parts)


def solution(mesh):
    spec = P(("seq", "outer"), None)
    return jax.shard_map(
        on_device, mesh=mesh, in_specs=(spec,) * 4, out_specs=(spec,) * 5, check_vma=False
    )
```

```python
import functools

import jax
import jax.numpy as jnp
from jax import lax
from jax.experimental import pallas as pl
from jax.experimental.pallas import tpu as pltpu
from jax.sharding import PartitionSpec as P

HEADS = 8
HEAD = 128
LEAF = 128
SPANS = 256
STEPS = 8
PLANE = 32
ZS, YS, XS = 8, 4, 4
GROUP = 2 * XS
AHEAD = 2
WINDOW = 5
HOLD = 4
HALF_LAG = 2
POST_LAG = 5
SCALE = HEAD**-0.5
LOG2E = 1.4426950408889634
MESH = pl.DeviceIdType.MESH
BF16 = jnp.bfloat16
F32 = jnp.float32

(
    S_TILE, S_RIM, S_PAIR, S_QUAD, S_QFWD, S_SUM, S_SFWD,
    S_RGRAD, S_PGRAD, S_QGRAD, S_HALF, S_XGRAD, S_BACK,
) = range(13)
R_RIM, R_PAIR, R_QUAD, R_QFWD, R_SUM, R_SFWD, R_RGRAD, R_PGRAD, R_QGRAD, R_HALF, R_XGRAD = range(11)


def dot(a, b, contract):
    return lax.dot_general(a, b, ((contract[:1], contract[1:]), ((), ())), preferred_element_type=F32)


def kernel(
    q_in, k_in, v_in, cot_in,
    att0, att1, gq0, gq1, gq2, gq3, gk0, gk1, gk2, gk3, gv0, gv1, gv2, gv3, sg,
    q, k, v, cot,
    tiles_in, sums, rim, pairs, pairs_in, quads, quads_in,
    rgrad, rgrad_in, pgrad, pgrad_in, qkeep, qgrad, qgrad_in,
    sgrad, half_in, xgrad, xgrad_in, probs_kept, dscores_kept, stage, back, back_in,
    send, recv, plane_recv, load,
):
    seq, outer = lax.axis_index("seq"), lax.axis_index("outer")
    x, ylo, z = lax.div(seq, 16), lax.rem(lax.div(seq, 8), 2), lax.rem(seq, 8)
    yhi, core = lax.div(outer, 2), lax.rem(outer, 2)
    span = seq * 4 + outer
    y = ylo * 2 + yhi
    member = z * 4 + y

    def at(x, y, z):
        return ((x * 2 + lax.div(y, 2)) * 8 + z, lax.rem(y, 2) * 2 + core)

    def of_span(s):
        return (lax.div(s, 4), lax.rem(s, 4))

    following = of_span(lax.rem(span + 1, SPANS))
    previous = of_span(lax.rem(span + SPANS - 1, SPANS))
    partner = (seq, yhi * 2 + 1 - core)
    sibling = (seq, (1 - yhi) * 2 + core)
    plane = [
        (lax.rem(z + dz, ZS) * YS + lax.rem(y + dy, YS), at(x, lax.rem(y + dy, YS), lax.rem(z + dz, ZS)))
        for dz in (4, 3, 5, 2, 6, 1, 7, 0)
        for dy in (2, 1, 3, 0)
        if dz or dy
    ]
    group = core * XS + x
    mates = [
        (there, ((there * 2 + ylo) * 8 + z, outer)) for there in (lax.rem(x + d, XS) for d in (2, 1, 3))
    ]

    loads = [
        pltpu.make_async_copy(src, dst, load.at[i])
        for i, (src, dst) in enumerate(((k_in, k), (v_in, v), (q_in, q), (cot_in, cot)))
    ]
    for copy in loads:
        copy.start()

    def post(src, dst, s, r, device):
        pltpu.make_async_remote_copy(
            src_ref=src, dst_ref=dst, send_sem=send.at[s], recv_sem=r, device_id=device, device_id_type=MESH
        ).start()

    def arrived(ref, sem):
        pltpu.make_async_copy(ref, ref, sem).wait()

    barrier = pltpu.get_barrier_semaphore()

    def greet(device):
        pl.semaphore_signal(barrier, inc=1, device_id=device, device_id_type=MESH)

    for _, device in plane + mates:
        greet(device)
    greet(partner)
    greet(following)
    greet(previous)

    def grid(rows, cols):
        return (
            lax.broadcasted_iota(jnp.int32, (rows, cols), 0),
            lax.broadcasted_iota(jnp.int32, (rows, cols), 1),
        )

    row, col = grid(128, 256)
    halve = jnp.where((col >> 1) == row, 0.5, 0.0).astype(BF16)
    row, col = grid(64, 128)
    halve_again = jnp.where((col >> 1) == row, 0.5, 0.0).astype(BF16)
    row, col = grid(256, 256)
    turn = jnp.where(col == ((row & 15) * 16 + (row >> 4)), 1.0, 0.0).astype(BF16)

    loads[0].wait()
    loads[1].wait()
    chunks = []
    for kv, ref in enumerate((k, v)):
        whole = ref[...]
        pair_rows = dot(halve, whole, (1, 0)).astype(BF16)
        quad_rows = dot(halve_again, pair_rows, (1, 0)).astype(BF16)
        mean = jnp.sum(whole.astype(F32), axis=0, keepdims=True) * (1.0 / 256)
        chunks += [mean[:, h * HEAD:(h + 1) * HEAD] for h in range(HEADS)]
        for t in range(STEPS):
            pairs[t, kv] = pair_rows[:, t * HEAD:(t + 1) * HEAD]
            quads[t, kv] = quad_rows[:, t * HEAD:(t + 1) * HEAD]
    tiles_in[member] = jnp.concatenate(chunks, axis=0).astype(BF16)

    pl.semaphore_wait(barrier, len(plane) + len(mates) + 3)

    for _, device in plane:
        post(tiles_in.at[member], tiles_in.at[member], S_TILE, plane_recv.at[0], device)

    def send_step(t, carry):
        cols = pl.ds(pl.multiple_of(t * HEAD, HEAD), HEAD)
        post(quads.at[t], quads_in.at[t, 0], S_QUAD, recv.at[R_QUAD, t], sibling)
        for kv, ref in enumerate((k_in, v_in)):
            post(ref.at[pl.ds(LEAF, LEAF), cols], rim.at[t, kv], S_RIM, recv.at[R_RIM, t], following)
            post(ref.at[pl.ds(0, LEAF), cols], rim.at[t, 2 + kv], S_RIM, recv.at[R_RIM, t], previous)
        post(pairs.at[t], pairs_in.at[t], S_PAIR, recv.at[R_PAIR, t], partner)
        return carry

    lax.fori_loop(0, STEPS, send_step, 0)

    arrived(tiles_in.at[pl.ds(0, PLANE - 1)], plane_recv.at[0])
    for part in range(2):
        turned = dot(turn, tiles_in[part * 16:(part + 1) * 16].reshape(256, HEAD), (1, 0)).astype(BF16)
        for t in range(STEPS):
            for kv in range(2):
                first = (kv * 8 + t) * 16
                sums[t, group, kv * 32 + part * 16:kv * 32 + (part + 1) * 16, :] = turned[first:first + 16]

    def send_sums(t, carry):
        for _, device in mates:
            post(sums.at[t, group], sums.at[t, group], S_SUM, recv.at[R_SUM, t], device)
        return carry

    lax.fori_loop(0, WINDOW, send_sums, 0)

    def forward(t):
        arrived(quads_in.at[t, 0], recv.at[R_QUAD, t])
        post(quads_in.at[t, 0], quads_in.at[t, 1], S_QFWD, recv.at[R_QFWD, t], partner)
        arrived(sums.at[t, pl.ds(0, XS - 1)], recv.at[R_SUM, t])
        four = sums.at[t, pl.ds(core * XS, XS)]
        post(four, four, S_SFWD, recv.at[R_SFWD, t], partner)

    for t in range(AHEAD):
        forward(t)
    loads[2].wait()
    loads[3].wait()

    row, col = grid(256, 256)
    covered = (((row >> 5) & 3) == x) & (((row & 31) >> 1) == z * 2 + ylo)
    row, col = grid(128, 256)
    absent = ((col < LEAF) & (span == 0)) | ((col >= LEAF) & (span == SPANS - 1))

    def columns(t):
        return pl.ds(pl.multiple_of(t * HEAD, HEAD), HEAD)

    def rows_of(t, kv, ref):
        return jnp.concatenate(
            [
                ref[:, columns(t)],
                pairs_in[t, kv],
                quads_in[t, 0, kv],
                quads_in[t, 1, kv],
                sums[t, :, kv * 32:(kv + 1) * 32, :].reshape(SPANS, HEAD),
            ],
            axis=0,
        )

    def send_rims(t):
        two, other_two = pl.ds(0, 2), pl.ds(2, 2)
        post(rgrad.at[t, two], rgrad_in.at[t, other_two], S_RGRAD, recv.at[R_RGRAD, t], previous)
        post(rgrad.at[t, other_two], rgrad_in.at[t, two], S_RGRAD, recv.at[R_RGRAD, t], following)

    def compute(t):
        @pl.when(t + WINDOW < STEPS)
        def _():
            send_sums(t + WINDOW, 0)

        @pl.when(t + AHEAD < STEPS)
        def _():
            forward(t + AHEAD)

        arrived(rim.at[t], recv.at[R_RIM, t])
        arrived(pairs_in.at[t], recv.at[R_PAIR, t])
        arrived(quads_in.at[t, 1], recv.at[R_QFWD, t])
        cols = columns(t)
        qh, ch = q[:, cols], cot[:, cols]

        def near(kv, ref, other):
            main = jnp.concatenate(
                [ref[:, cols], pairs_in[t, kv], quads_in[t, 0, kv], quads_in[t, 1, kv]], axis=0
            )
            at_rim = jnp.concatenate(
                [dot(rim[t, kv], other[:LEAF], (1, 1)), dot(rim[t, 2 + kv], other[LEAF:], (1, 1))], axis=1
            )
            return dot(main, other, (1, 1)), at_rim

        def far(kv, other):
            return dot(sums[t, :, kv * 32:(kv + 1) * 32, :].reshape(SPANS, HEAD), other, (1, 1))

        near_scores, rim_scores = near(0, k, qh)
        near_dprobs, rim_dprobs = near(1, v, ch)
        arrived(sums.at[t, pl.ds(0, XS)], recv.at[R_SFWD, t])
        scores = jnp.concatenate(
            [near_scores, jnp.where(covered, -1e30, far(0, qh)), jnp.where(absent, -1e30, rim_scores)], axis=0
        )
        highest = jnp.max(scores, axis=0, keepdims=True)
        weights = jnp.exp2((scores - highest) * (SCALE * LOG2E))
        probs = weights * (1.0 / jnp.sum(weights, axis=0, keepdims=True))
        probs_low = probs.astype(BF16)
        dprobs = jnp.concatenate([near_dprobs, far(1, ch), rim_dprobs], axis=0)
        centre = jnp.sum(probs * dprobs, axis=0, keepdims=True)
        dscores = (probs * (dprobs - centre)).astype(BF16)

        probs_kept[t] = probs_low
        dscores_kept[t] = dscores

        sides = ((dscores, qh, SCALE), (probs_low, ch, 1.0))
        for kv, (low, other, factor) in enumerate(sides):
            far = (dot(low[512:768], other, (1, 0)) * factor).astype(BF16)
            sgrad[t, :, kv * 32:(kv + 1) * 32, :] = far.reshape(GROUP, 32, HEAD)
        post(sgrad.at[t, pl.ds((1 - core) * XS, XS)], half_in.at[t], S_HALF, recv.at[R_HALF, t], partner)

        for kv, (low, other, factor) in enumerate(sides):
            rgrad[t, kv] = (dot(low[768:, :LEAF], other[:LEAF], (1, 0)) * factor).astype(BF16)
            rgrad[t, 2 + kv] = (dot(low[768:, LEAF:], other[LEAF:], (1, 0)) * factor).astype(BF16)
        @pl.when(t < HOLD)
        def _():
            send_rims(t)

        for kv, (low, other, factor) in enumerate(sides):
            coarse = dot(low[256:512], other, (1, 0)) * factor
            pgrad[t, kv, 0:128, :] = coarse[:128].astype(BF16)
            qkeep[t, kv] = coarse[128:192]
            pgrad[t, kv, 128:192, :] = coarse[192:].astype(BF16)
        post(pgrad.at[t], pgrad_in.at[t], S_PGRAD, recv.at[R_PGRAD, t], partner)

    def gathered(t, kv, ref, weights):
        total = dot(rows_of(t, kv, ref), weights[:768], (0, 0))
        at_rim = jnp.concatenate(
            [
                dot(rim[t, kv], weights[768:, :LEAF], (0, 0)),
                dot(rim[t, 2 + kv], weights[768:, LEAF:], (0, 0)),
            ],
            axis=1,
        )
        return (total + at_rim).T

    def put(t, refs, value):
        each = STEPS // len(refs)
        for i, ref in enumerate(refs):
            @pl.when(lax.div(t, each) == i)
            def _(ref=ref):
                ref[:, columns(lax.rem(t, each))] = value

    def gather(t):
        put(t, (att0, att1), gathered(t, 1, v, probs_kept[t]).astype(BF16))
        put(t, (gq0, gq1, gq2, gq3), gathered(t, 0, k, dscores_kept[t]) * SCALE)

    def halves(t):
        arrived(half_in.at[t], recv.at[R_HALF, t])
        own = sgrad[t, pl.ds(core * XS, XS)].astype(F32)
        xgrad[t] = (own + half_in[t].astype(F32)).astype(BF16)
        for there, device in mates:
            post(xgrad.at[t, there], xgrad_in.at[t, x], S_XGRAD, recv.at[R_XGRAD, t], device)
        xgrad_in[t, x] = xgrad[t, x]
        arrived(pgrad_in.at[t], recv.at[R_PGRAD, t])
        qgrad[t] = (qkeep[t] + pgrad_in[t, :, 128:192, :].astype(F32)).astype(BF16)
        post(qgrad.at[t], qgrad_in.at[t], S_QGRAD, recv.at[R_QGRAD, t], sibling)

    def reduce(t):
        arrived(xgrad_in.at[t, pl.ds(0, XS - 1)], recv.at[R_XGRAD, t])
        total = jnp.sum(xgrad_in[t].astype(F32), axis=0).astype(BF16)
        for kv in range(2):
            for part in range(2):
                first = kv * 32 + part * 16
                stage[part, kv * 8 + t] = total[first:first + 16]

    row, col = grid(256, 128)
    double = jnp.where((row >> 1) == col, 0.5, 0.0).astype(BF16)
    row, col = grid(256, 64)
    double_twice = jnp.where((row >> 2) == col, 0.25, 0.0).astype(BF16)

    def join(t):
        arrived(rgrad_in.at[t], recv.at[R_RGRAD, t])
        arrived(qgrad_in.at[t], recv.at[R_QGRAD, t])
        cols = columns(t)
        sides = ((dscores_kept, q, (gk0, gk1, gk2, gk3), SCALE), (probs_kept, cot, (gv0, gv1, gv2, gv3), 1.0))
        for kv, (low, other, out, factor) in enumerate(sides):
            own = dot(low[t, 0:256, :], other[:, cols], (1, 0)) * factor
            ends = jnp.concatenate([rgrad_in[t, kv], rgrad_in[t, 2 + kv]], axis=0).astype(F32)
            coarse = dot(double, pgrad_in[t, kv, 0:128, :], (1, 0)) + dot(double_twice, qgrad_in[t, kv], (1, 0))
            put(t, out, own + ends + coarse)

    def step(t, carry):
        compute(t)

        @pl.when(t >= HALF_LAG)
        def _():
            halves(t - HALF_LAG)

        @pl.when(t >= POST_LAG)
        def _():
            reduce(t - POST_LAG)

        return carry

    def repeat(f):
        def body(t, carry):
            f(t)
            return carry

        return body

    lax.fori_loop(0, STEPS, step, 0)
    lax.fori_loop(STEPS - HALF_LAG, STEPS, repeat(halves), 0)
    lax.fori_loop(STEPS - POST_LAG, STEPS, repeat(reduce), 0)

    for part in range(2):
        turned = dot(turn, stage[part].reshape(256, HEAD), (1, 0)).astype(BF16)
        back[part * 16:(part + 1) * 16] = turned.reshape(16, 16, HEAD)
    for there, device in plane:
        post(back.at[there], back_in.at[member], S_BACK, plane_recv.at[1], device)
    back_in[member] = back[member]
    lax.fori_loop(HOLD, STEPS, repeat(send_rims), 0)

    lax.fori_loop(0, STEPS, repeat(gather), 0)
    lax.fori_loop(0, STEPS, repeat(join), 0)
    arrived(back_in.at[pl.ds(0, PLANE - 1)], plane_recv.at[1])
    total = jnp.sum(back_in[...].astype(F32), axis=0)
    for c in range(2 * HEADS):
        sg[:, c * HEAD:(c + 1) * HEAD] = total[c:c + 1]

    arrived(tiles_in.at[pl.ds(0, PLANE - 1)], send.at[S_TILE])
    arrived(rim, send.at[S_RIM])
    arrived(pairs, send.at[S_PAIR])
    arrived(quads, send.at[S_QUAD])
    arrived(quads, send.at[S_QFWD])
    arrived(sums.at[:, pl.ds(0, XS - 1)], send.at[S_SUM])
    arrived(sums.at[:, pl.ds(0, XS)], send.at[S_SFWD])
    arrived(rgrad, send.at[S_RGRAD])
    arrived(pgrad, send.at[S_PGRAD])
    arrived(qgrad, send.at[S_QGRAD])
    arrived(half_in, send.at[S_HALF])
    arrived(xgrad.at[:, pl.ds(0, XS - 1)], send.at[S_XGRAD])
    arrived(back.at[pl.ds(0, PLANE - 1)], send.at[S_BACK])


def finish(*refs):
    pieces, sg, outs, (kept, sem) = refs[:14], refs[14], refs[15:20], refs[20:]
    copies = [pltpu.make_async_copy(sg, outs[4], sem.at[14])]
    copies[0].start()
    for i, piece in enumerate(pieces):
        out, at = (outs[0], i) if i < 2 else (outs[1 + (i - 2) // 4], (i - 2) % 4)
        width = piece.shape[1]
        if i >= 6:
            kept[i - 6] = piece[...] + sg[:, (i - 6) * width:(i - 5) * width] * (1.0 / 256)
            piece = kept.at[i - 6]
        copies.append(pltpu.make_async_copy(piece, out.at[:, pl.ds(at * width, width)], sem.at[i]))
        copies[-1].start()
    for copy in copies:
        copy.wait()


def on_device(queries, keys, values, cotangent):
    rows, width = queries.shape
    in_vmem = pl.BlockSpec(memory_space=pltpu.VMEM)
    in_hbm = pl.BlockSpec(memory_space=pltpu.HBM)
    out_shape = (
        jax.ShapeDtypeStruct((rows, width), BF16),
        jax.ShapeDtypeStruct((rows, width), F32),
        jax.ShapeDtypeStruct((rows, width), F32),
        jax.ShapeDtypeStruct((rows, width), F32),
        jax.ShapeDtypeStruct((1, 2 * width), F32),
    )
    pieces = (
        [jax.ShapeDtypeStruct((rows, width // 2), BF16)] * 2
        + [jax.ShapeDtypeStruct((rows, width // 4), F32)] * 12
        + [jax.ShapeDtypeStruct((1, 2 * width), F32)]
    )
    block = (STEPS, 4, LEAF, HEAD)
    parts = pl.pallas_call(
        kernel,
        out_shape=pieces,
        in_specs=[in_hbm] * 4,
        out_specs=[in_vmem] * 15,
        scratch_shapes=[pltpu.VMEM((rows, width), BF16)] * 4 + [
            pltpu.VMEM((PLANE, 16, HEAD), BF16),
            pltpu.VMEM((STEPS, GROUP, 64, HEAD), BF16),
            pltpu.VMEM(block, BF16),
            pltpu.VMEM((STEPS, 2, 128, HEAD), BF16),
            pltpu.VMEM((STEPS, 2, 128, HEAD), BF16),
            pltpu.VMEM((STEPS, 2, 64, HEAD), BF16),
            pltpu.VMEM((STEPS, 2, 2, 64, HEAD), BF16),
            pltpu.VMEM(block, BF16),
            pltpu.VMEM(block, BF16),
            pltpu.VMEM((STEPS, 2, 192, HEAD), BF16),
            pltpu.VMEM((STEPS, 2, 192, HEAD), BF16),
            pltpu.VMEM((STEPS, 2, 64, HEAD), F32),
            pltpu.VMEM((STEPS, 2, 64, HEAD), BF16),
            pltpu.VMEM((STEPS, 2, 64, HEAD), BF16),
            pltpu.VMEM((STEPS, GROUP, 64, HEAD), BF16),
            pltpu.VMEM((STEPS, XS, 64, HEAD), BF16),
            pltpu.VMEM((STEPS, XS, 64, HEAD), BF16),
            pltpu.VMEM((STEPS, XS, 64, HEAD), BF16),
            pltpu.VMEM((STEPS, 896, 256), BF16),
            pltpu.VMEM((STEPS, 896, 256), BF16),
            pltpu.VMEM((2, 16, 16, HEAD), BF16),
            pltpu.VMEM((PLANE, 16, HEAD), BF16),
            pltpu.VMEM((PLANE, 16, HEAD), BF16),
            pltpu.SemaphoreType.DMA((13,)),
            pltpu.SemaphoreType.DMA((11, STEPS)),
            pltpu.SemaphoreType.DMA((2,)),
            pltpu.SemaphoreType.DMA((4,)),
        ],
        compiler_params=pltpu.CompilerParams(
            collective_id=0, has_side_effects=True, vmem_limit_bytes=50 * 2**20
        ),
        name="attend",
    )(queries, keys, values, cotangent)
    return pl.pallas_call(
        finish,
        out_shape=out_shape,
        in_specs=[in_vmem] * 15,
        out_specs=(in_hbm,) * 5,
        scratch_shapes=[
            pltpu.VMEM((8, rows, width // 4), F32),
            pltpu.SemaphoreType.DMA((15,)),
        ],
        compiler_params=pltpu.CompilerParams(vmem_limit_bytes=16 * 2**20),
        name="finish",
    )(*parts)


def solution(mesh):
    spec = P(("seq", "outer"), None)
    return jax.shard_map(
        on_device, mesh=mesh, in_specs=(spec,) * 4, out_specs=(spec,) * 5, check_vma=False
    )
```
